512 devices in a mesh: img: 16 (over y_lo, x), blk: 32 (over y_hi, z, core).
Axes of the slice: x: 4, y: 8 (y_hi: 2, y_lo: 4; y = y_hi * 4 + y_lo), z: 8, core: 2. Of those that a mesh axis runs over, the one named last changes fastest.
Arguments:
- jac_cam: bfloat16 [16, 32, 1536, 128], P('img', 'blk')
- jac_tex: bfloat16 [16, 32, 1536, 256], P('img', 'blk')
- residual: bfloat16 [16, 32, 1536], P('img', 'blk'), may hold values from -6 to 6
- obs_slot: int32 [16, 32, 192], P('img', 'blk'), may hold values from 0 to 15, never falling along the last dimension, each value on 1 to 36 neighbouring positions
- col_ids: int32 [512], P('blk'), may hold values from 0 to 511, each once
- block_pattern: int32 [512], replicated, may hold values from 0 to 3, as said below
- damping: float32 [], replicated, may hold values from 0.1 to 1
Outputs:
- reduced_blocks: float32 [32, 16, 128, 128], P('blk', 'img')
- reduced_gradient: float32 [32, 16, 128], P('blk', 'img')
- coupling_factor: float32 [32, 16, 128, 256], P('blk', 'img')
- texture_factor: float32 [256, 256], replicated
The draws below stay inside these ranges and needn't reach their ends.
Inputs may be any that keep to these rules, and one draw needn't show every extreme that they name: `obs_slot`: Non-decreasing along each device's observations; every slot 0 to 15 has 1 to 36 observations on every device, and some slot exactly 36. `col_ids`: each global block column appears once. `block_pattern`: bit 0 marks coupling with texture panel 0, bit 1 with panel 1; exactly 128 columns carry code 1, exactly 128 carry code 2, exactly 2 carry code 0, and all others code 3.
All inputs are finite; a program needn't handle non-finite values.
Results may differ from the reference program's by a relative error of at most 0.00095.
Values sent between devices are 32-bit elements; how exact they have to be, the bound alone decides.
No kernel may reach another device: no remote copies, remote signals or barrier semaphores. Data moves between devices by JAX's collectives and lax.ppermute only.
A program may use at most 64 MiB of HBM per device.

```python
import math
import jax
import jax.numpy as jnp
import numpy as np
from jax import lax

BLOCK = 128
TEX_W = 256
OBS_DEV = 192
NBD = 16
UNCOUPLED = 2
MOST = 36
ROWS_DEV = 1536
GROUPS = 16
OWNERS = 32
NB = 512


def shared_normal(key):
    return jax.random.normal(jax.random.fold_in(key, 1), (GROUPS, OWNERS, ROWS_DEV, BLOCK), jnp.float32)


def shared_column(key):
    return jax.random.normal(jax.random.fold_in(key, 3), (GROUPS, OWNERS, ROWS_DEV, 1), jnp.float32)


def row_scale(key):
    spread = jax.random.uniform(jax.random.fold_in(key, 2), (GROUPS, OWNERS, ROWS_DEV, 1), jnp.float32, 0.0, math.log(10.0))
    return jnp.exp(spread) * (ROWS_DEV * GROUPS / NBD * 21.5) ** (-0.5)


def device_rise():
    flat = (jnp.arange(GROUPS)[:, None] * OWNERS + jnp.arange(OWNERS)[None, :]).astype(jnp.float32)
    ramp = flat / (GROUPS * OWNERS - 1)
    return ((1.0 + 3.0 * ramp) / math.sqrt(7.0))[:, :, None, None]


def draw_jac_cam(key, part):
    base = shared_normal(key)
    common = shared_column(key)
    scaled = row_scale(key)
    return ((base + common) * scaled).astype(jnp.bfloat16)


def draw_jac_tex(key, part):
    base = shared_normal(key)
    common = shared_column(key)
    scaled = row_scale(key) * device_rise()
    key = jax.random.fold_in(key, 47)
    weight = 0.5
    first = 0.8 * base + 0.6 * jax.random.normal(jax.random.fold_in(key, 1), base.shape, jnp.float32) + weight * common
    second = 0.6 * base + 0.8 * jax.random.normal(jax.random.fold_in(key, 2), base.shape, jnp.float32) + weight * common
    return (jnp.concatenate([first, second], axis=-1) * scaled).astype(jnp.bfloat16)


def draw_block_pattern(key, part):
    key = jax.random.fold_in(key, 5)
    positions = jnp.arange(NB).astype(jnp.int32)
    quarter = NB // 4
    ordered = jnp.where(positions < UNCOUPLED, 0, jnp.where(positions < UNCOUPLED + quarter, 1, jnp.where(positions < UNCOUPLED + 2 * quarter, 2, 3))).astype(jnp.int32)
    return jax.random.permutation(key, ordered).astype(jnp.int32)


def levels(rng, shape, pieces, smallest, high):
    gain, own = 1.0, jax.random.fold_in(rng, 6)
    for position, shards_of in pieces:
        heights = jnp.exp(jax.random.uniform(jax.random.fold_in(own, position), (shards_of,), jnp.float32, smallest / len(pieces), high / len(pieces)))
        gain = gain * jnp.repeat(heights, shape[position] // shards_of).reshape([-1 if axis == position else 1 for axis in range(len(shape))])
    return gain


def profile(amount, total, bound, skew):
    portions = [(1 << 20) // math.isqrt(rank ** skew) + 1 for rank in range(2, amount + 1)]
    surplus, holding = total - bound - (amount - 1), [1] * (amount - 1)
    while surplus > 0:
        candidates = [i for i in range(amount - 1) if holding[i] < bound]
        mass, left = sum([portions[i] for i in candidates]), surplus
        for i in candidates:
            extra = min(bound - holding[i], max(1, left * portions[i] // mass), surplus)
            holding[i] = holding[i] + extra
            surplus = surplus - extra
    return np.array([bound] + holding)


def ragged(rng, amount, total, most, lean):
    if amount == 2:
        one = jax.random.randint(rng, (), max(1, total - most), min(most, total - 1) + 1)
        return jnp.stack([one, total - one])
    sizes = jnp.asarray(profile(amount, total, most, lean), jnp.int32)
    pairs = (amount - 1) // 2
    source_of, receiver = sizes[1:1 + 2 * pairs:2], sizes[2:2 + 2 * pairs:2]
    slack = jnp.minimum(source_of - 1, most - receiver)
    moved = jax.random.randint(jax.random.fold_in(rng, 1), (pairs,), 0, 1 << 20) % (slack + 1)
    sizes = sizes.at[1:1 + 2 * pairs:2].set(source_of - moved).at[2:2 + 2 * pairs:2].set(receiver + moved)
    return sizes[jax.random.permutation(jax.random.fold_in(rng, 2), amount)]


def normal_values(stream_key, extent, scale, reach, split=(), kind=jnp.bfloat16):
    gain = levels(stream_key, extent, split, -0.22, 0.18) if split else 1.0
    values = jax.random.normal(stream_key, extent, jnp.float32) * scale * gain
    return jnp.minimum(jnp.maximum(values, -reach), reach).astype(kind)


def setup_inputs(seed: int = 0) -> dict:
    splits = jax.random.split(jax.random.key(seed), 8)
    return {
        "jac_cam": draw_jac_cam(jax.random.fold_in(splits[7], 71), 0),
        "jac_tex": draw_jac_tex(jax.random.fold_in(splits[7], 71), 0),
        "residual": normal_values(splits[2], (GROUPS, OWNERS, ROWS_DEV), 1.0, 6.0, ((0, 16), (1, 32))),
        "obs_slot": jax.vmap(lambda own: jnp.searchsorted(jnp.cumsum(ragged(own, NBD, OBS_DEV, MOST, 2)), jnp.arange(OBS_DEV), side="right"))(jax.random.split(splits[3], GROUPS * OWNERS)).reshape((GROUPS, OWNERS, OBS_DEV)).astype(jnp.int32),
        "col_ids": jax.random.permutation(splits[4], NB).astype(jnp.int32),
        "block_pattern": draw_block_pattern(jax.random.fold_in(splits[7], 71), 0),
        "damping": jnp.clip(jnp.exp(jax.random.uniform(splits[6], (), jnp.float32, math.log(0.1), math.log(1.0))), 0.1, 1.0),
    }


def exact_dot(left, right):
    return jnp.dot(left.astype(jnp.float32), right.astype(jnp.float32), precision=lax.Precision.HIGHEST, preferred_element_type=jnp.float32)

def tri_inverse(lower_factor):
    identity = jnp.eye(lower_factor.shape[0], dtype=jnp.float32)
    return lax.linalg.triangular_solve(lower_factor, identity, left_side=True, lower=True)

def device_partial(jac_cam, jac_tex, residual, obs_slot, slot_codes):
    row_count = jac_cam.shape[0]
    repeat_count = row_count // obs_slot.shape[0]
    slot_count = slot_codes.shape[0]
    slot_range = jnp.arange(slot_count).astype(jnp.int32)
    row_slot = jnp.repeat(obs_slot, repeat_count)
    onehot = row_slot[:, None] == slot_range[None, :]
    row_code = jnp.sum(jnp.where(onehot, slot_codes[None, :], 0), axis=1)
    half_cols = jac_tex.shape[1] // 2
    keep_first = row_code % 2 == 1
    keep_second = row_code // 2 == 1
    col_first = jnp.arange(jac_tex.shape[1]) < half_cols
    keep = jnp.where(col_first[None, :], keep_first[:, None], keep_second[:, None])
    masked_tex = jnp.where(keep, jac_tex, jnp.zeros_like(jac_tex))
    tex_hess = jnp.dot(masked_tex.T.astype(jnp.float32), masked_tex.astype(jnp.float32), preferred_element_type=jnp.float32)
    tex_grad = jnp.dot(residual.astype(jnp.float32), masked_tex.astype(jnp.float32), preferred_element_type=jnp.float32)
    starts = jnp.sum((obs_slot[None, :] < slot_range[:, None]).astype(jnp.int32), axis=1) * repeat_count
    window_rows = min(MOST * repeat_count, row_count)

    def one_slot(slot_index):
        window_start = jnp.minimum(starts[slot_index], row_count - window_rows).astype(jnp.int32)
        cam_rows = lax.dynamic_slice_in_dim(jac_cam, window_start, window_rows, 0)
        tex_rows = lax.dynamic_slice_in_dim(masked_tex, window_start, window_rows, 0)
        res_rows = lax.dynamic_slice_in_dim(residual, window_start, window_rows, 0)
        row_match = lax.dynamic_slice_in_dim(row_slot, window_start, window_rows, 0) == slot_index
        picked = jnp.where(row_match[:, None], cam_rows, jnp.zeros_like(cam_rows))
        cam_hess = jnp.dot(picked.T.astype(jnp.float32), cam_rows.astype(jnp.float32), preferred_element_type=jnp.float32)
        cam_cross = jnp.dot(picked.T.astype(jnp.float32), tex_rows.astype(jnp.float32), preferred_element_type=jnp.float32)
        cam_grad = jnp.dot(res_rows.astype(jnp.float32), picked.astype(jnp.float32), preferred_element_type=jnp.float32)
        return (cam_hess, cam_cross, cam_grad)
    cam_hess, cam_cross, cam_grad = lax.map(one_slot, slot_range)
    return (cam_hess, cam_cross, cam_grad, tex_hess, tex_grad)

def damp_texture(tex_hess, damping):
    return tex_hess + damping * jnp.diag(jnp.diagonal(tex_hess))

def first_panel(damped, tex_grad):
    half_cols = damped.shape[0] // 2
    low_first = jnp.linalg.cholesky(damped[:half_cols, :half_cols])
    inv_first = tri_inverse(low_first)
    low_cross = exact_dot(damped[half_cols:, :half_cols], inv_first.T)
    sol_first = exact_dot(inv_first, tex_grad[:half_cols])
    return (low_first, low_cross, inv_first, sol_first)

def second_panel(damped, tex_grad, low_cross, inv_first, sol_first):
    half_cols = damped.shape[0] // 2
    updated = damped[half_cols:, half_cols:] - exact_dot(low_cross, low_cross.T)
    low_second = jnp.linalg.cholesky(updated)
    inv_second = tri_inverse(low_second)
    inv_cross = -exact_dot(inv_second, exact_dot(low_cross, inv_first))
    sol_second = exact_dot(inv_second, tex_grad[half_cols:] - exact_dot(low_cross, sol_first))
    return (low_second, inv_second, inv_cross, sol_second)

def reference(jac_cam, jac_tex, residual, obs_slot, col_ids, block_pattern, damping):
    slot_codes = block_pattern[col_ids].reshape(OWNERS, NBD)

    def per_owner(owner):

        def add_group(total, group):
            partial_sums = device_partial(jac_cam[group, owner], jac_tex[group, owner], residual[group, owner], obs_slot[group, owner], slot_codes[owner])
            return (tuple((left + right for left, right in zip(total, partial_sums))), None)
        start_value = (jnp.zeros((NBD, BLOCK, BLOCK), jnp.float32), jnp.zeros((NBD, BLOCK, TEX_W), jnp.float32), jnp.zeros((NBD, BLOCK), jnp.float32), jnp.zeros((TEX_W, TEX_W), jnp.float32), jnp.zeros((TEX_W,), jnp.float32))
        result, unused = lax.scan(add_group, start_value, jnp.arange(GROUPS).astype(jnp.int32))
        return result
    cam_hess, cam_cross, cam_grad, tex_parts, grad_parts = lax.map(per_owner, jnp.arange(OWNERS).astype(jnp.int32))
    tex_hess = jnp.sum(tex_parts, axis=0)
    tex_grad = jnp.sum(grad_parts, axis=0)
    damped = damp_texture(tex_hess, damping)
    low_first, low_cross, inv_first, sol_first = first_panel(damped, tex_grad)
    low_second, inv_second, inv_cross, sol_second = second_panel(damped, tex_grad, low_cross, inv_first, sol_first)
    blank = jnp.zeros((BLOCK, BLOCK), jnp.float32)
    texture_factor = jnp.concatenate([jnp.concatenate([low_first, blank], 1), jnp.concatenate([low_cross, low_second], 1)], 0)
    inverse = jnp.concatenate([jnp.concatenate([inv_first, blank], 1), jnp.concatenate([inv_cross, inv_second], 1)], 0)
    solution = jnp.concatenate([sol_first, sol_second], 0)
    coupling = jnp.einsum('oabp,qp->oabq', cam_cross, inverse, precision=lax.Precision.HIGHEST)
    identity = jnp.eye(BLOCK, dtype=jnp.float32)
    reduced = cam_hess + damping * (cam_hess * identity) - jnp.einsum('oabp,oacp->oabc', coupling, coupling, precision=lax.Precision.HIGHEST)
    gradient = cam_grad - jnp.einsum('oabp,p->oab', coupling, solution, precision=lax.Precision.HIGHEST)
    return (reduced, gradient, coupling, texture_factor)
```

```python
import functools

import jax
import jax.numpy as jnp
from jax import lax
from jax.experimental import pallas as pl
from jax.experimental.pallas import tpu as pltpu
from jax.sharding import Mesh, PartitionSpec as P

BLOCK = 128
TEX_W = 256
ROWS = 1536
OBS = 192
PER = 8
SLOTS = 16
PIECE = 328
F32 = jnp.float32
VMEM = pl.BlockSpec(memory_space=pltpu.VMEM)
SMEM = pl.BlockSpec(memory_space=pltpu.SMEM)


def col_dot(left, right):
    return lax.dot_general(left, right, (((0,), (0,)), ((), ())), preferred_element_type=F32)


def exact_dot(left, right, dims=((1,), (0,))):
    return lax.dot_general(
        left, right, (dims, ((), ())), precision=lax.Precision.HIGHEST, preferred_element_type=F32
    )


def iota(shape, dim):
    return lax.broadcasted_iota(jnp.int32, shape, dim)


def find_starts(obs_ref, starts):
    starts[SLOTS] = OBS

    def step(i, carry):
        j = OBS - 1 - i
        starts[obs_ref[j]] = j
        return carry

    lax.fori_loop(0, OBS, step, 0, unroll=8)


def tex_kernel(tex_ref, res_ref, obs_ref, ids_ref, pattern_ref, out_ref, starts):
    find_starts(obs_ref, starts)
    obs_index = iota((OBS, BLOCK), 0)
    masks = []
    for bit in range(2):
        keep = jnp.zeros((OBS, BLOCK), jnp.int32)
        before = jnp.int32(0)
        for s in range(SLOTS):
            now = (pattern_ref[ids_ref[s]] >> bit) & 1
            keep = jnp.where(obs_index >= starts[s], now, keep)
            before = now
        keep = keep.astype(F32)
        rows = jnp.broadcast_to(keep[:, None, :], (OBS, PER, BLOCK)).reshape(ROWS, BLOCK)
        masks.append(rows.astype(jnp.bfloat16))
    masked = tex_ref[...] * jnp.concatenate(masks, axis=1)
    hess = col_dot(masked, masked)
    grad = jnp.dot(res_ref[...], masked, preferred_element_type=F32)
    h00, h10, h11 = hess[:BLOCK, :BLOCK], hess[BLOCK:, :BLOCK], hess[BLOCK:, BLOCK:]
    row, col = iota((BLOCK, BLOCK), 0), iota((BLOCK, BLOCK), 1)
    mixed = jnp.where(row >= col, h00, h11)
    diag = jnp.sum(jnp.where(row == col, h11, 0.0), axis=0, keepdims=True)
    out_ref[...] = jnp.zeros(out_ref.shape, F32)
    out_ref[:16, :8, :] = mixed.reshape(16, 8, BLOCK)
    out_ref[16:, :8, :] = h10.reshape(16, 8, BLOCK)
    out_ref[0, 8:9, :] = grad[:, :BLOCK]
    out_ref[1, 8:9, :] = grad[:, BLOCK:]
    out_ref[2, 8:9, :] = diag


def cam_kernel(cam_ref, tex_ref, res_ref, obs_ref, ids_ref, pattern_ref, place_ref, *rest):
    outs, starts = rest[:4], rest[4]
    find_starts(obs_ref, starts)
    my_yl, my_x = place_ref[0], place_ref[1]
    row64, lane64 = iota((64, BLOCK), 0), iota((64, BLOCK), 1)
    row256 = iota((256, BLOCK), 0)
    row48 = iota((48, BLOCK), 0)
    sub = iota((SLOTS, BLOCK), 0)
    first = jnp.zeros((SLOTS, BLOCK), jnp.int32)
    last = jnp.zeros((SLOTS, BLOCK), jnp.int32)
    for k in range(4):
        for j in range(4):
            out = outs[k]
            base = j * PIECE
            slot = ((my_yl + j) & 3) * 4 + ((my_x + k) & 3)
            lo, hi = starts[slot] * PER, starts[slot + 1] * PER
            code = pattern_ref[ids_ref[slot]]
            first = jnp.where(sub == k * 4 + j, lo, first)
            last = jnp.where(sub == k * 4 + j, hi, last)
            begin = jnp.minimum((lo >> 4) << 4, ROWS - 256)
            begin = pl.multiple_of(begin, 16)

            def part(begin, low, rows, count):
                cam = cam_ref[pl.ds(begin, count), :]
                tex = tex_ref[pl.ds(begin, count), :]
                where = rows + begin
                keep = ((where >= low) & (where < hi)).astype(F32).astype(jnp.bfloat16)
                picked = cam * keep
                return col_dot(picked, cam), col_dot(picked, tex)

            hess, cross = part(begin, lo, row256, 256)
            keep0, keep1 = (code & 1) == 1, (code >> 1) == 1
            zero = jnp.zeros((BLOCK, BLOCK), F32)

            def packed(hess):
                low, high = hess[64:, :], hess[:64, :]
                turned = pltpu.roll(high, 64, 1)
                pair = jnp.where((lane64 >= 64) & (row64 >= lane64 - 64), turned, low)
                diag = jnp.sum(jnp.where(row64 == lane64 - 64, low, 0.0), axis=0, keepdims=True)
                return pair, diag

            pair, diag = packed(hess)
            out[base : base + 128, :] = jnp.where(keep0, cross[:, :BLOCK], zero)
            out[base + 128 : base + 256, :] = jnp.where(keep1, cross[:, BLOCK:], zero)
            out[base + 256 : base + 320, :] = pair
            out[base + 320 : base + 328, :] = jnp.broadcast_to(diag, (8, BLOCK))

            @pl.when(hi > begin + 256)
            def _():
                second = jnp.minimum(begin + 256, ROWS - 48)
                second = pl.multiple_of(second, 16)
                hess, cross = part(second, begin + 256, row48, 48)
                pair, diag = packed(hess)
                out[base : base + 128, :] += jnp.where(keep0, cross[:, :BLOCK], zero)
                out[base + 128 : base + 256, :] += jnp.where(keep1, cross[:, BLOCK:], zero)
                out[base + 256 : base + 320, :] += pair
                out[base + 320 : base + 328, :] += jnp.broadcast_to(diag, (8, BLOCK))

    lane = iota((SLOTS, ROWS), 1)
    first = jnp.tile(first, (1, ROWS // BLOCK))
    last = jnp.tile(last, (1, ROWS // BLOCK))
    res = jnp.broadcast_to(res_ref[...].astype(F32), (SLOTS, ROWS))
    spread = jnp.where((lane >= first) & (lane < last), res, 0.0).astype(jnp.bfloat16)
    grad = jnp.dot(spread, cam_ref[...], preferred_element_type=F32)
    for k in range(4):
        for j in range(4):
            base = j * PIECE
            outs[k][base + 320 : base + 321, :] = grad[k * 4 + j : k * 4 + j + 1, :]


def add_kernel(a_ref, b_ref, c_ref, d_ref, *outs):
    for j in range(4):
        rows = slice(j * PIECE, (j + 1) * PIECE)
        outs[j][...] = (a_ref[rows, :] + b_ref[rows, :]) + (c_ref[rows, :] + d_ref[rows, :])


def factor(a):
    row, col = iota((BLOCK, BLOCK), 0), iota((BLOCK, BLOCK), 1)
    eye = (row == col).astype(F32)

    def step(j, carry):
        a, b, low = carry
        pick = col == j
        column = jnp.sum(jnp.where(pick, a, 0.0), axis=1, keepdims=True)
        here = row[:, :1] == j
        pivot = jnp.sum(jnp.where(here, column, 0.0), axis=0, keepdims=True)
        scale = lax.rsqrt(pivot)
        arow = jnp.sum(jnp.where(row == j, a, 0.0), axis=0, keepdims=True) * scale
        brow = jnp.sum(jnp.where(row == j, b, 0.0), axis=0, keepdims=True) * scale
        column = jnp.where(row[:, :1] >= j, column, 0.0) * scale
        low = jnp.where(pick, column, low)
        under = jnp.where(here, 0.0, column)
        a = a - under * arow
        b = jnp.where(row == j, brow, b - under * brow)
        return a, b, low

    a, b, low = lax.fori_loop(0, BLOCK, step, (a, eye, jnp.zeros((BLOCK, BLOCK), F32)))
    return low, b


def panel_kernel(sums_ref, damping_ref, factor_ref, inv_ref, sol_ref):
    damping = damping_ref[0]
    sums = sums_ref[...]
    both = sums[:, :8, :].reshape(TEX_W, BLOCK)
    mixed, h10 = both[:BLOCK], both[BLOCK:]
    g0, g1, diag = sums[0, 8:9, :], sums[1, 8:9, :], sums[2, 8:9, :]
    row, col = iota((BLOCK, BLOCK), 0), iota((BLOCK, BLOCK), 1)
    flipped = mixed.T
    h00 = jnp.where(row >= col, mixed, flipped)
    h11 = jnp.where(row < col, mixed, jnp.where(row == col, diag, flipped))
    h00 = jnp.where(row == col, h00 + damping * h00, h00)
    h11 = jnp.where(row == col, h11 + damping * h11, h11)
    l00, w00 = factor(h00)
    l10 = exact_dot(h10, w00, ((1,), (1,)))
    y0 = exact_dot(g0, w00, ((1,), (1,)))
    l11, w11 = factor(h11 - exact_dot(l10, l10, ((1,), (1,))))
    w10 = -exact_dot(w11, exact_dot(l10, w00))
    y1 = exact_dot(g1 - exact_dot(y0, l10, ((1,), (1,))), w11, ((1,), (1,)))
    zero = jnp.zeros((BLOCK, BLOCK), F32)
    factor_ref[:BLOCK, :BLOCK] = l00
    factor_ref[:BLOCK, BLOCK:] = zero
    factor_ref[BLOCK:, :BLOCK] = l10
    factor_ref[BLOCK:, BLOCK:] = l11
    inv_ref[:BLOCK, :BLOCK] = w00
    inv_ref[:BLOCK, BLOCK:] = zero
    inv_ref[BLOCK:, :BLOCK] = w10
    inv_ref[BLOCK:, BLOCK:] = w11
    sol_ref[:, :BLOCK] = y0
    sol_ref[:, BLOCK:] = y1


def last_kernel(a_ref, b_ref, c_ref, d_ref, inv_ref, sol_ref, damping_ref, red_ref, grad_ref, coup_ref):
    damping = damping_ref[0]
    total = (a_ref[...] + b_ref[...]) + (c_ref[...] + d_ref[...])
    cross = jnp.concatenate([total[:128], total[128:256]], axis=1)
    pair, grad, diag = total[256:320], total[320:321], total[321:322]
    row, col = iota((BLOCK, BLOCK), 0), iota((BLOCK, BLOCK), 1)
    row64, lane64 = iota((64, BLOCK), 0), iota((64, BLOCK), 1)
    turned = pltpu.roll(pair, 64, 1)
    top = jnp.where(lane64 < 64, turned, 0.0)
    square = jnp.concatenate([top, pair], axis=0)
    other = square.T
    lower = jnp.where((row >= 64) & (col >= 64), other, square)
    lower = jnp.where(row > col, lower, 0.0)
    main = jnp.where(row == col, jnp.where(row < 64, square, diag), 0.0)
    hess = lower + lower.T + main + damping * main
    coupling = exact_dot(cross, inv_ref[...], ((1,), (1,)))
    coup_ref[...] = coupling
    red_ref[...] = hess - exact_dot(coupling, coupling, ((1,), (1,)))
    grad_ref[...] = grad - exact_dot(sol_ref[...], coupling, ((1,), (1,)))


def call(kernel, name, outs, specs, scratch=()):
    return pl.pallas_call(
        kernel,
        out_shape=[jax.ShapeDtypeStruct(s, F32) for s in outs],
        in_specs=specs,
        out_specs=[VMEM] * len(outs),
        scratch_shapes=scratch,
        name=name,
        compiler_params=pltpu.CompilerParams(vmem_limit_bytes=24 * 2**20),
    )


def spread_sum(value, axes):
    count = lax.axis_size(axes)
    copies = jnp.broadcast_to(value[None], (count, *value.shape))
    return jnp.sum(lax.all_to_all(copies, axes, 0, 0), axis=0)


def shift(value, axis, by):
    n = lax.axis_size(axis)
    return lax.ppermute(value, axis, [(i, (i + by) % n) for i in range(n)])


FAR = ("x", "z")
NEAR = ("yl", "yh", "c")


def shards(jac_cam, jac_tex, residual, obs_slot, col_ids, block_pattern, damping):
    cam, tex = jac_cam[0, 0], jac_tex[0, 0]
    res, obs = residual[0], obs_slot[0, 0]
    damping = damping.reshape(1)
    starts = [pltpu.SMEM((SLOTS + 1,), jnp.int32)]
    place = jnp.stack([lax.axis_index("yl"), lax.axis_index("x")]).astype(jnp.int32)

    (tex_part,) = call(
        tex_kernel, "tex", [(32, 16, BLOCK)], [VMEM, VMEM, SMEM, SMEM, SMEM], starts
    )(tex, res, obs, col_ids, block_pattern)
    share = jnp.sum(lax.all_to_all(tex_part, FAR, 0, 0), axis=0)
    share = spread_sum(share, NEAR)
    copies = jnp.broadcast_to(share[None], (32, *share.shape))
    tex_sums = lax.all_to_all(copies, FAR, 0, 0)

    pieces = call(
        cam_kernel,
        "cam",
        [(4 * PIECE, BLOCK)] * 4,
        [VMEM, VMEM, VMEM, SMEM, SMEM, SMEM, SMEM],
        starts,
    )(cam, tex, res, obs, col_ids, block_pattern, place)
    moved = [pieces[0]] + [shift(pieces[k], "x", k) for k in (1, 2, 3)]
    pieces = call(add_kernel, "add", [(PIECE, BLOCK)] * 4, [VMEM] * 4)(*moved)
    moved = [pieces[0]] + [shift(pieces[j], "yl", j) for j in (1, 2, 3)]

    texture_factor, inverse, sol = call(
        panel_kernel, "panel", [(TEX_W, TEX_W), (TEX_W, TEX_W), (1, TEX_W)], [VMEM, SMEM]
    )(tex_sums, damping)
    reduced, gradient, coupling = call(
        last_kernel,
        "last",
        [(BLOCK, BLOCK), (1, BLOCK), (BLOCK, TEX_W)],
        [VMEM] * 6 + [SMEM],
    )(*moved, inverse, sol, damping)
    return (reduced[None, None], gradient[None], coupling[None, None], texture_factor)


def solution(mesh):
    fine = Mesh(mesh.devices.reshape(4, 4, 2, 8, 2), ("yl", "x", "yh", "z", "c"))
    img, blk = ("yl", "x"), ("yh", "z", "c")
    return jax.shard_map(
        shards,
        mesh=fine,
        in_specs=(
            P(img, blk, None, None),
            P(img, blk, None, None),
            P(img, blk, None),
            P(img, blk, None),
            P(blk),
            P(),
            P(),
        ),
        out_specs=(
            P(blk, img, None, None),
            P(blk, img, None),
            P(blk, img, None, None),
            P(),
        ),
        check_vma=False,
    )
```

```python
import functools

import jax
import jax.numpy as jnp
from jax import lax
from jax.experimental import pallas as pl
from jax.experimental.pallas import tpu as pltpu
from jax.sharding import Mesh, PartitionSpec as P

BLOCK = 128
TEX_W = 256
ROWS = 1536
OBS = 192
PER = 8
SLOTS = 16
PIECE = 328
F32 = jnp.float32
VMEM = pl.BlockSpec(memory_space=pltpu.VMEM)
HBM = pl.BlockSpec(memory_space=pltpu.HBM)
SMEM = pl.BlockSpec(memory_space=pltpu.SMEM)


def col_dot(left, right):
    return lax.dot_general(left, right, (((0,), (0,)), ((), ())), preferred_element_type=F32)


def exact_dot(left, right, dims=((1,), (0,))):
    return lax.dot_general(
        left, right, (dims, ((), ())), precision=lax.Precision.HIGHEST, preferred_element_type=F32
    )


def iota(shape, dim):
    return lax.broadcasted_iota(jnp.int32, shape, dim)


def find_starts(obs_ref, starts):
    starts[SLOTS] = OBS

    def step(i, carry):
        j = OBS - 1 - i
        starts[obs_ref[j]] = j
        return carry

    lax.fori_loop(0, OBS, step, 0, unroll=8)


def tex_sums(tex_ref, res_ref, ids_ref, pattern_ref, starts, out_ref):
    obs_index = iota((OBS, BLOCK), 0)
    masks = []
    for bit in range(2):
        keep = jnp.zeros((OBS, BLOCK), jnp.int32)
        for s in range(SLOTS):
            keep = jnp.where(obs_index >= starts[s], (pattern_ref[ids_ref[s]] >> bit) & 1, keep)
        rows = jnp.broadcast_to(keep.astype(F32)[:, None, :], (OBS, PER, BLOCK))
        masks.append(rows.reshape(ROWS, BLOCK).astype(jnp.bfloat16))
    masked = tex_ref[...] * jnp.concatenate(masks, axis=1)
    hess = col_dot(masked, masked)
    grad = jnp.dot(res_ref[...], masked, preferred_element_type=F32)
    h00, h10, h11 = hess[:BLOCK, :BLOCK], hess[BLOCK:, :BLOCK], hess[BLOCK:, BLOCK:]
    row, col = iota((BLOCK, BLOCK), 0), iota((BLOCK, BLOCK), 1)
    mixed = jnp.where(row >= col, h00, h11)
    diag = jnp.sum(jnp.where(row == col, h11, 0.0), axis=0, keepdims=True)
    out_ref[:, 8:, :] = jnp.zeros((32, 8, BLOCK), F32)
    out_ref[:16, :8, :] = mixed.reshape(16, 8, BLOCK)
    out_ref[16:, :8, :] = h10.reshape(16, 8, BLOCK)
    out_ref[0, 8:9, :] = grad[:, :BLOCK]
    out_ref[1, 8:9, :] = grad[:, BLOCK:]
    out_ref[2, 8:9, :] = diag


def packed(hess):
    row, lane = iota((64, BLOCK), 0), iota((64, BLOCK), 1)
    low, high = hess[64:, :], hess[:64, :]
    turned = pltpu.roll(high, 64, 1)
    pair = jnp.where((lane >= 64) & (row >= lane - 64), turned, low)
    return pair, jnp.sum(jnp.where(row == lane - 64, low, 0.0), axis=0, keepdims=True)


def local_kernel(
    cam_any, tex_any, res_any, obs_any, ids_any, pattern_any, out, tex_out,
    starts, cam_ref, tex_ref, res_ref, obs_ref, ids_ref, pattern_ref, sems, small,
):
    near = [
        pltpu.make_async_copy(src, dst, small.at[i])
        for i, (src, dst) in enumerate(
            ((obs_any, obs_ref), (ids_any, ids_ref), (pattern_any, pattern_ref), (res_any, res_ref))
        )
    ]
    for copy in near:
        copy.start()
    copies = []
    for i, (src, dst) in enumerate(((cam_any, cam_ref), (tex_any, tex_ref))):
        for n in range(4):
            rows = pl.ds(n * (ROWS // 4), ROWS // 4)
            copies.append(pltpu.make_async_copy(src.at[rows, :], dst.at[rows, :], sems.at[i * 4 + n]))
    for copy in copies:
        copy.start()
    for copy in near:
        copy.wait()
    find_starts(obs_ref, starts)
    sub = iota((SLOTS, BLOCK), 0)
    first = jnp.zeros((SLOTS, BLOCK), jnp.int32)
    last = jnp.zeros((SLOTS, BLOCK), jnp.int32)
    for copy in copies:
        copy.wait()
    tex_sums(tex_ref, res_ref, ids_ref, pattern_ref, starts, tex_out)

    def bounds(k, j):
        slot = j * 4 + k
        lo, hi = starts[slot] * PER, starts[slot + 1] * PER
        begin = pl.multiple_of(jnp.minimum((lo >> 4) << 4, ROWS - 256), 16)
        code = pattern_ref[ids_ref[slot]]
        return lo, hi, begin, (code & 1) == 1, (code >> 1) == 1

    def part(begin, lo, hi, count):
        cam = cam_ref[pl.ds(begin, count), :]
        both = jnp.concatenate([cam, tex_ref[pl.ds(begin, count), :]], axis=1)
        where = iota((count, BLOCK), 0) + begin
        keep = ((where >= lo) & (where < hi)).astype(F32).astype(jnp.bfloat16)
        return col_dot(cam * keep, both)

    zero = jnp.zeros((BLOCK, BLOCK), F32)
    for k in range(4):
        for j in range(4):
            base = (k * 4 + j) * PIECE
            lo, hi, begin, keep0, keep1 = bounds(k, j)
            first = jnp.where(sub == k * 4 + j, lo, first)
            last = jnp.where(sub == k * 4 + j, hi, last)
            sums = part(begin, lo, hi, 256)
            pair, diag = packed(sums[:, :BLOCK])
            out[base : base + 128, :] = jnp.where(keep0, sums[:, BLOCK : 2 * BLOCK], zero)
            out[base + 128 : base + 256, :] = jnp.where(keep1, sums[:, 2 * BLOCK :], zero)
            out[base + 256 : base + 320, :] = pair
            out[base + 320 : base + 328, :] = jnp.broadcast_to(diag, (8, BLOCK))

    lane = iota((SLOTS, ROWS), 1)
    first = jnp.tile(first, (1, ROWS // BLOCK))
    last = jnp.tile(last, (1, ROWS // BLOCK))
    res = jnp.broadcast_to(res_ref[...].astype(F32), (SLOTS, ROWS))
    spread = jnp.where((lane >= first) & (lane < last), res, 0.0).astype(jnp.bfloat16)
    grad = jnp.dot(spread, cam_ref[...], preferred_element_type=F32)
    for i in range(SLOTS):
        out[i * PIECE + 320 : i * PIECE + 321, :] = grad[i : i + 1, :]

    for k in range(4):
        for j in range(4):
            base = (k * 4 + j) * PIECE
            lo, hi, begin, keep0, keep1 = bounds(k, j)

            @pl.when(hi > begin + 256)
            def _():
                second = pl.multiple_of(jnp.minimum(begin + 256, ROWS - 48), 16)
                sums = part(second, begin + 256, hi, 48)
                pair, diag = packed(sums[:, :BLOCK])
                out[base : base + 128, :] += jnp.where(keep0, sums[:, BLOCK : 2 * BLOCK], zero)
                out[base + 128 : base + 256, :] += jnp.where(keep1, sums[:, 2 * BLOCK :], zero)
                out[base + 256 : base + 320, :] += pair
                out[base + 321 : base + 322, :] += diag


def split3(value):
    high = value.astype(jnp.bfloat16)
    return high, (value - high.astype(F32)).astype(jnp.bfloat16)


def near_dot(left, right, dims=((1,), (0,))):
    (lk,), (rk,) = dims
    lh, ll = split3(left)
    rh, rl = split3(right)
    return lax.dot_general(
        jnp.concatenate([lh, lh, ll], axis=lk),
        jnp.concatenate([rh, rl, rh], axis=rk),
        (dims, ((), ())),
        preferred_element_type=F32,
    )


def lanes(value, k):
    return jnp.broadcast_to(value[:, k : k + 1], (8, BLOCK))


def subs(value, j):
    return jnp.broadcast_to(value[j : j + 1, :], (8, BLOCK))


def factor(ab, upper, block):
    row, col = iota((BLOCK, BLOCK), 0), iota((BLOCK, BLOCK), 1)
    sub = iota((8, BLOCK), 0)
    ab[:, :BLOCK] = block
    ab[:, BLOCK:] = (row == col).astype(F32)
    cur = [block[:8], ab[:8, BLOCK:]]
    for b in range(16):
        more = b < 15
        heads = [lanes(cur[0], 8 * b + k) for k in range(8)]
        if more:
            rows = slice(8 * (b + 1), 8 * (b + 2))
            below = [ab[rows, :BLOCK], ab[rows, BLOCK:]]
            tails = [lanes(below[0], 8 * b + k) for k in range(8)]
        for j in range(8):
            scale = lax.rsqrt(subs(heads[j], j))
            head = jnp.where(sub > j, heads[j] * scale, 0.0)
            for k in range(j + 1, 8):
                pick = subs(heads[k], j) * scale
                heads[k] = heads[k] - head * pick
                if more:
                    if k == j + 1:
                        tail = tails[j] * scale
                    tails[k] = tails[k] - tail * pick
            if more and j == 7:
                tail = tails[j] * scale
            for part in range(2):
                pivot = subs(cur[part], j) * scale
                cur[part] = jnp.where(sub == j, pivot, cur[part] - head * pivot)
                if more:
                    below[part] = below[part] - tail * pivot
        done = jnp.concatenate(cur, axis=1)
        upper[8 * b : 8 * b + 8, :] = done
        if b < 14:
            high, low = split3(done)
            update = col_dot(
                jnp.concatenate([high[:, :BLOCK], high[:, :BLOCK], low[:, :BLOCK]], axis=0),
                jnp.concatenate([high, low, high], axis=0),
            )
            ab[8 * (b + 2) :, :] -= update[8 * (b + 2) :, :]
        if more:
            cur = below
    return jnp.where(row >= col, upper[:, :BLOCK].T, 0.0), upper[:, BLOCK:]


def panel_kernel(sums_ref, damping_ref, factor_ref, inv_ref, sol_ref, ab, upper):
    damping = damping_ref[0]
    sums = sums_ref[...]
    both = sums[:, :8, :].reshape(TEX_W, BLOCK)
    mixed, h10 = both[:BLOCK], both[BLOCK:]
    g0, g1, diag = sums[0, 8:9, :], sums[1, 8:9, :], sums[2, 8:9, :]
    row, col = iota((BLOCK, BLOCK), 0), iota((BLOCK, BLOCK), 1)
    flipped = mixed.T
    h00 = jnp.where(row >= col, mixed, flipped)
    h11 = jnp.where(row < col, mixed, jnp.where(row == col, diag, flipped))
    h00 = jnp.where(row == col, h00 + damping * h00, h00)
    h11 = jnp.where(row == col, h11 + damping * h11, h11)
    across = ((1,), (1,))
    l00, w00 = factor(ab, upper, h00)
    l10 = near_dot(h10, w00, across)
    y0 = near_dot(g0, w00, across)
    zero = jnp.zeros((BLOCK, BLOCK), F32)
    factor_ref[:BLOCK, :BLOCK] = l00
    factor_ref[:BLOCK, BLOCK:] = zero
    factor_ref[BLOCK:, :BLOCK] = l10
    inv_ref[:BLOCK, :BLOCK] = w00
    inv_ref[:BLOCK, BLOCK:] = zero
    lw = near_dot(l10, w00)
    l11, w11 = factor(ab, upper, h11 - near_dot(l10, l10, across))
    factor_ref[BLOCK:, BLOCK:] = l11
    inv_ref[BLOCK:, :BLOCK] = -near_dot(w11, lw)
    inv_ref[BLOCK:, BLOCK:] = w11
    sol_ref[:, :BLOCK] = y0
    sol_ref[:, BLOCK:] = near_dot(g1 - near_dot(y0, l10, across), w11, across)


def last_kernel(parts_ref, inv_ref, sol_ref, damping_ref, red_ref, grad_ref, coup_ref):
    damping = damping_ref[0]
    total = (parts_ref[0] + parts_ref[1]) + (parts_ref[2] + parts_ref[3])
    cross = jnp.concatenate([total[:128], total[128:256]], axis=1)
    pair, grad, diag = total[256:320], total[320:321], total[321:322]
    row, col = iota((BLOCK, BLOCK), 0), iota((BLOCK, BLOCK), 1)
    row64, lane64 = iota((64, BLOCK), 0), iota((64, BLOCK), 1)
    turned = pltpu.roll(pair, 64, 1)
    top = jnp.where(lane64 < 64, turned, 0.0)
    square = jnp.concatenate([top, pair], axis=0)
    other = square.T
    lower = jnp.where((row >= 64) & (col >= 64), other, square)
    lower = jnp.where(row > col, lower, 0.0)
    main = jnp.where(row == col, jnp.where(row < 64, square, diag), 0.0)
    hess = lower + lower.T + main + damping * main
    coupling = exact_dot(cross, inv_ref[...], ((1,), (1,)))
    coup_ref[...] = coupling
    red_ref[...] = hess - exact_dot(coupling, coupling, ((1,), (1,)))
    grad_ref[...] = grad - exact_dot(sol_ref[...], coupling, ((1,), (1,)))


LOCAL_SCRATCH = [
    pltpu.SMEM((SLOTS + 1,), jnp.int32),
    pltpu.VMEM((ROWS, BLOCK), jnp.bfloat16),
    pltpu.VMEM((ROWS, TEX_W), jnp.bfloat16),
    pltpu.VMEM((1, ROWS), jnp.bfloat16),
    pltpu.SMEM((OBS,), jnp.int32),
    pltpu.SMEM((SLOTS,), jnp.int32),
    pltpu.SMEM((512,), jnp.int32),
    pltpu.SemaphoreType.DMA((8,)),
    pltpu.SemaphoreType.DMA((4,)),
]
PANEL = [pltpu.VMEM((BLOCK, TEX_W), F32), pltpu.VMEM((BLOCK, TEX_W), F32)]


def call(kernel, name, outs, specs, scratch=(), room=24):
    return pl.pallas_call(
        kernel,
        out_shape=[jax.ShapeDtypeStruct(s, F32) for s in outs],
        in_specs=specs,
        out_specs=[VMEM] * len(outs),
        scratch_shapes=scratch,
        name=name,
        compiler_params=pltpu.CompilerParams(vmem_limit_bytes=room * 2**20),
    )


def spread_sum(value, axes):
    count = lax.axis_size(axes)
    copies = jnp.broadcast_to(value[None], (count, *value.shape))
    return jnp.sum(lax.all_to_all(copies, axes, 0, 0), axis=0)


FAR = ("x", "z")
NEAR = ("yl", "yh", "c")


def shards(jac_cam, jac_tex, residual, obs_slot, col_ids, block_pattern, damping):
    cam, tex = jac_cam[0, 0], jac_tex[0, 0]
    res, obs = residual[0], obs_slot[0, 0]
    damping = damping.reshape(1)

    cam_part, tex_part = call(
        local_kernel, "local", [(16 * PIECE, BLOCK), (32, 16, BLOCK)], [HBM] * 6, LOCAL_SCRATCH, 60
    )(cam, tex, res, obs, col_ids, block_pattern)

    share = jnp.sum(lax.all_to_all(tex_part, FAR, 0, 0), axis=0)
    share = spread_sum(share, NEAR)
    copies = jnp.broadcast_to(share[None], (32, *share.shape))
    tex_sums = lax.all_to_all(copies, FAR, 0, 0)

    pieces = lax.psum_scatter(cam_part, "x", scatter_dimension=0, tiled=True)
    parts = lax.all_to_all(pieces.reshape(4, PIECE, BLOCK), "yl", 0, 0)

    texture_factor, inverse, sol = call(
        panel_kernel, "panel", [(TEX_W, TEX_W), (TEX_W, TEX_W), (1, TEX_W)], [VMEM, SMEM], PANEL
    )(tex_sums, damping)
    reduced, gradient, coupling = call(
        last_kernel,
        "last",
        [(BLOCK, BLOCK), (1, BLOCK), (BLOCK, TEX_W)],
        [VMEM] * 3 + [SMEM],
    )(parts, inverse, sol, damping)
    return (reduced[None, None], gradient[None], coupling[None, None], texture_factor)


def solution(mesh):
    fine = Mesh(mesh.devices.reshape(4, 4, 2, 8, 2), ("yl", "x", "yh", "z", "c"))
    img, blk = ("yl", "x"), ("yh", "z", "c")
    return jax.shard_map(
        shards,
        mesh=fine,
        in_specs=(
            P(img, blk, None, None),
            P(img, blk, None, None),
            P(img, blk, None),
            P(img, blk, None),
            P(blk),
            P(),
            P(),
        ),
        out_specs=(
            P(blk, img, None, None),
            P(blk, img, None),
            P(blk, img, None, None),
            P(),
        ),
        check_vma=False,
    )
```

```python
import functools

import jax
import jax.numpy as jnp
from jax import lax
from jax.experimental import pallas as pl
from jax.experimental.pallas import tpu as pltpu
from jax.sharding import Mesh, PartitionSpec as P

BLOCK = 128
TEX_W = 256
ROWS = 1536
OBS = 192
PER = 8
SLOTS = 16
PIECE = 328
F32 = jnp.float32
VMEM = pl.BlockSpec(memory_space=pltpu.VMEM)
HBM = pl.BlockSpec(memory_space=pltpu.HBM)
SMEM = pl.BlockSpec(memory_space=pltpu.SMEM)


def col_dot(left, right):
    return lax.dot_general(left, right, (((0,), (0,)), ((), ())), preferred_element_type=F32)


def exact_dot(left, right, dims=((1,), (0,))):
    return lax.dot_general(
        left, right, (dims, ((), ())), precision=lax.Precision.HIGHEST, preferred_element_type=F32
    )


def iota(shape, dim):
    return lax.broadcasted_iota(jnp.int32, shape, dim)


def find_starts(obs_ref, starts):
    starts[SLOTS] = OBS

    def step(i, carry):
        j = OBS - 1 - i
        starts[obs_ref[j]] = j
        return carry

    lax.fori_loop(0, OBS, step, 0, unroll=8)


def tex_sums(tex_ref, res_ref, ids_ref, pattern_ref, starts, out_ref):
    obs_index = iota((OBS, BLOCK), 0)
    masks = []
    for bit in range(2):
        keep = jnp.zeros((OBS, BLOCK), jnp.int32)
        for s in range(SLOTS):
            keep = jnp.where(obs_index >= starts[s], (pattern_ref[ids_ref[s]] >> bit) & 1, keep)
        rows = jnp.broadcast_to(keep.astype(F32)[:, None, :], (OBS, PER, BLOCK))
        masks.append(rows.reshape(ROWS, BLOCK).astype(jnp.bfloat16))
    masked = tex_ref[...] * jnp.concatenate(masks, axis=1)
    hess = col_dot(masked, masked)
    grad = jnp.dot(res_ref[...], masked, preferred_element_type=F32)
    h00, h10, h11 = hess[:BLOCK, :BLOCK], hess[BLOCK:, :BLOCK], hess[BLOCK:, BLOCK:]
    row, col = iota((BLOCK, BLOCK), 0), iota((BLOCK, BLOCK), 1)
    mixed = jnp.where(row >= col, h00, h11)
    diag = jnp.sum(jnp.where(row == col, h11, 0.0), axis=0, keepdims=True)
    out_ref[:, 16:, :] = jnp.zeros((16, 8, BLOCK), F32)
    out_ref[:8, :16, :] = mixed.reshape(8, 16, BLOCK)
    out_ref[8:, :16, :] = h10.reshape(8, 16, BLOCK)
    out_ref[0, 16:17, :] = grad[:, :BLOCK]
    out_ref[1, 16:17, :] = grad[:, BLOCK:]
    out_ref[2, 16:17, :] = diag


def packed(hess):
    row, lane = iota((64, BLOCK), 0), iota((64, BLOCK), 1)
    low, high = hess[64:, :], hess[:64, :]
    turned = pltpu.roll(high, 64, 1)
    pair = jnp.where((lane >= 64) & (row >= lane - 64), turned, low)
    return pair, jnp.sum(jnp.where(row == lane - 64, low, 0.0), axis=0, keepdims=True)


def local_kernel(
    cam_any, tex_any, res_any, obs_any, ids_any, pattern_any, out0, out1, out2, out3, tex_out,
    starts, cam_ref, tex_ref, res_ref, obs_ref, ids_ref, pattern_ref, sems, small,
):
    outs, my_x = (out0, out1, out2, out3), lax.axis_index("x")
    near = [
        pltpu.make_async_copy(src, dst, small.at[i])
        for i, (src, dst) in enumerate(
            ((obs_any, obs_ref), (ids_any, ids_ref), (pattern_any, pattern_ref), (res_any, res_ref))
        )
    ]
    for copy in near:
        copy.start()
    copies = []
    for i, (src, dst) in enumerate(((cam_any, cam_ref), (tex_any, tex_ref))):
        for n in range(4):
            rows = pl.ds(n * (ROWS // 4), ROWS // 4)
            copies.append(pltpu.make_async_copy(src.at[rows, :], dst.at[rows, :], sems.at[i * 4 + n]))
    for copy in copies:
        copy.start()
    for copy in near:
        copy.wait()
    find_starts(obs_ref, starts)
    sub = iota((SLOTS, BLOCK), 0)
    first = jnp.zeros((SLOTS, BLOCK), jnp.int32)
    last = jnp.zeros((SLOTS, BLOCK), jnp.int32)
    for copy in copies:
        copy.wait()
    tex_sums(tex_ref, res_ref, ids_ref, pattern_ref, starts, tex_out)

    def bounds(k, j):
        slot = j * 4 + ((my_x + k) & 3)
        lo, hi = starts[slot] * PER, starts[slot + 1] * PER
        begin = pl.multiple_of(jnp.minimum((lo >> 4) << 4, ROWS - 256), 16)
        code = pattern_ref[ids_ref[slot]]
        return lo, hi, begin, (code & 1) == 1, (code >> 1) == 1

    def part(begin, lo, hi, count):
        cam = cam_ref[pl.ds(begin, count), :]
        both = jnp.concatenate([cam, tex_ref[pl.ds(begin, count), :]], axis=1)
        where = iota((count, BLOCK), 0) + begin
        keep = ((where >= lo) & (where < hi)).astype(F32).astype(jnp.bfloat16)
        return col_dot(cam * keep, both)

    zero = jnp.zeros((BLOCK, BLOCK), F32)
    for k in range(4):
        for j in range(4):
            out, base = outs[k], j * PIECE
            lo, hi, begin, keep0, keep1 = bounds(k, j)
            first = jnp.where(sub == k * 4 + j, lo, first)
            last = jnp.where(sub == k * 4 + j, hi, last)
            sums = part(begin, lo, hi, 256)
            pair, diag = packed(sums[:, :BLOCK])
            out[base : base + 128, :] = jnp.where(keep0, sums[:, BLOCK : 2 * BLOCK], zero)
            out[base + 128 : base + 256, :] = jnp.where(keep1, sums[:, 2 * BLOCK :], zero)
            out[base + 256 : base + 320, :] = pair
            out[base + 320 : base + 328, :] = jnp.broadcast_to(diag, (8, BLOCK))

    lane = iota((SLOTS, ROWS), 1)
    first = jnp.tile(first, (1, ROWS // BLOCK))
    last = jnp.tile(last, (1, ROWS // BLOCK))
    res = jnp.broadcast_to(res_ref[...].astype(F32), (SLOTS, ROWS))
    spread = jnp.where((lane >= first) & (lane < last), res, 0.0).astype(jnp.bfloat16)
    grad = jnp.dot(spread, cam_ref[...], preferred_element_type=F32)
    for i in range(SLOTS):
        base = (i % 4) * PIECE
        outs[i // 4][base + 320 : base + 321, :] = grad[i : i + 1, :]

    for k in range(4):
        for j in range(4):
            out, base = outs[k], j * PIECE
            lo, hi, begin, keep0, keep1 = bounds(k, j)

            @pl.when(hi > begin + 256)
            def _():
                second = pl.multiple_of(jnp.minimum(begin + 256, ROWS - 48), 16)
                sums = part(second, begin + 256, hi, 48)
                pair, diag = packed(sums[:, :BLOCK])
                out[base : base + 128, :] += jnp.where(keep0, sums[:, BLOCK : 2 * BLOCK], zero)
                out[base + 128 : base + 256, :] += jnp.where(keep1, sums[:, 2 * BLOCK :], zero)
                out[base + 256 : base + 320, :] += pair
                out[base + 321 : base + 322, :] += diag


def add_kernel(a_ref, b_ref, c_ref, d_ref, out_ref):
    out_ref[...] = (a_ref[...] + b_ref[...]) + (c_ref[...] + d_ref[...])


def split3(value):
    high = value.astype(jnp.bfloat16)
    return high, (value - high.astype(F32)).astype(jnp.bfloat16)


def near_dot(left, right, dims=((1,), (0,))):
    (lk,), (rk,) = dims
    lh, ll = split3(left)
    rh, rl = split3(right)
    return lax.dot_general(
        jnp.concatenate([lh, lh, ll], axis=lk),
        jnp.concatenate([rh, rl, rh], axis=rk),
        (dims, ((), ())),
        preferred_element_type=F32,
    )


def lanes(value, k):
    return jnp.broadcast_to(value[:, k : k + 1], (8, BLOCK))


def subs(value, j):
    return jnp.broadcast_to(value[j : j + 1, :], (8, BLOCK))


def factor(ab, upper, block):
    row, col = iota((BLOCK, BLOCK), 0), iota((BLOCK, BLOCK), 1)
    sub = iota((8, BLOCK), 0)
    ab[:, :BLOCK] = block
    ab[:, BLOCK:] = (row == col).astype(F32)
    cur = [block[:8], ab[:8, BLOCK:]]
    for b in range(16):
        more = b < 15
        heads = [lanes(cur[0], 8 * b + k) for k in range(8)]
        if more:
            rows = slice(8 * (b + 1), 8 * (b + 2))
            below = [ab[rows, :BLOCK], ab[rows, BLOCK:]]
            tails = [lanes(below[0], 8 * b + k) for k in range(8)]
        for j in range(8):
            scale = lax.rsqrt(subs(heads[j], j))
            head = jnp.where(sub > j, heads[j] * scale, 0.0)
            for k in range(j + 1, 8):
                pick = subs(heads[k], j) * scale
                heads[k] = heads[k] - head * pick
                if more:
                    if k == j + 1:
                        tail = tails[j] * scale
                    tails[k] = tails[k] - tail * pick
            if more and j == 7:
                tail = tails[j] * scale
            for part in range(2):
                pivot = subs(cur[part], j) * scale
                cur[part] = jnp.where(sub == j, pivot, cur[part] - head * pivot)
                if more:
                    below[part] = below[part] - tail * pivot
        done = jnp.concatenate(cur, axis=1)
        upper[8 * b : 8 * b + 8, :] = done
        if b < 14:
            high, low = split3(done)
            update = col_dot(
                jnp.concatenate([high[:, :BLOCK], high[:, :BLOCK], low[:, :BLOCK]], axis=0),
                jnp.concatenate([high, low, high], axis=0),
            )
            ab[8 * (b + 2) :, :] -= update[8 * (b + 2) :, :]
        if more:
            cur = below
    return jnp.where(row >= col, upper[:, :BLOCK].T, 0.0), upper[:, BLOCK:]


def panel_kernel(sums_ref, damping_ref, factor_ref, inv_ref, sol_ref, ab, upper):
    damping = damping_ref[0]
    sums = sums_ref[...]
    both = sums[:, :16, :].reshape(TEX_W, BLOCK)
    mixed, h10 = both[:BLOCK], both[BLOCK:]
    g0, g1, diag = sums[0, 16:17, :], sums[1, 16:17, :], sums[2, 16:17, :]
    row, col = iota((BLOCK, BLOCK), 0), iota((BLOCK, BLOCK), 1)
    flipped = mixed.T
    h00 = jnp.where(row >= col, mixed, flipped)
    h11 = jnp.where(row < col, mixed, jnp.where(row == col, diag, flipped))
    h00 = jnp.where(row == col, h00 + damping * h00, h00)
    h11 = jnp.where(row == col, h11 + damping * h11, h11)
    across = ((1,), (1,))
    l00, w00 = factor(ab, upper, h00)
    l10 = near_dot(h10, w00, across)
    y0 = near_dot(g0, w00, across)
    zero = jnp.zeros((BLOCK, BLOCK), F32)
    factor_ref[:BLOCK, :BLOCK] = l00
    factor_ref[:BLOCK, BLOCK:] = zero
    factor_ref[BLOCK:, :BLOCK] = l10
    inv_ref[:BLOCK, :BLOCK] = w00
    inv_ref[:BLOCK, BLOCK:] = zero
    lw = near_dot(l10, w00)
    l11, w11 = factor(ab, upper, h11 - near_dot(l10, l10, across))
    factor_ref[BLOCK:, BLOCK:] = l11
    inv_ref[BLOCK:, :BLOCK] = -near_dot(w11, lw)
    inv_ref[BLOCK:, BLOCK:] = w11
    sol_ref[:, :BLOCK] = y0
    sol_ref[:, BLOCK:] = near_dot(g1 - near_dot(y0, l10, across), w11, across)


def last_kernel(parts_ref, inv_ref, sol_ref, damping_ref, red_ref, grad_ref, coup_ref):
    damping = damping_ref[0]
    total = (parts_ref[0] + parts_ref[1]) + (parts_ref[2] + parts_ref[3])
    cross = jnp.concatenate([total[:128], total[128:256]], axis=1)
    pair, grad, diag = total[256:320], total[320:321], total[321:322]
    row, col = iota((BLOCK, BLOCK), 0), iota((BLOCK, BLOCK), 1)
    row64, lane64 = iota((64, BLOCK), 0), iota((64, BLOCK), 1)
    turned = pltpu.roll(pair, 64, 1)
    top = jnp.where(lane64 < 64, turned, 0.0)
    square = jnp.concatenate([top, pair], axis=0)
    other = square.T
    lower = jnp.where((row >= 64) & (col >= 64), other, square)
    lower = jnp.where(row > col, lower, 0.0)
    main = jnp.where(row == col, jnp.where(row < 64, square, diag), 0.0)
    hess = lower + lower.T + main + damping * main
    coupling = exact_dot(cross, inv_ref[...], ((1,), (1,)))
    coup_ref[...] = coupling
    red_ref[...] = hess - exact_dot(coupling, coupling, ((1,), (1,)))
    grad_ref[...] = grad - exact_dot(sol_ref[...], coupling, ((1,), (1,)))


LOCAL_SCRATCH = [
    pltpu.SMEM((SLOTS + 1,), jnp.int32),
    pltpu.VMEM((ROWS, BLOCK), jnp.bfloat16),
    pltpu.VMEM((ROWS, TEX_W), jnp.bfloat16),
    pltpu.VMEM((1, ROWS), jnp.bfloat16),
    pltpu.SMEM((OBS,), jnp.int32),
    pltpu.SMEM((SLOTS,), jnp.int32),
    pltpu.SMEM((512,), jnp.int32),
    pltpu.SemaphoreType.DMA((8,)),
    pltpu.SemaphoreType.DMA((4,)),
]
PANEL = [pltpu.VMEM((BLOCK, TEX_W), F32), pltpu.VMEM((BLOCK, TEX_W), F32)]


def call(kernel, name, outs, specs, scratch=(), room=24):
    return pl.pallas_call(
        kernel,
        out_shape=[jax.ShapeDtypeStruct(s, F32) for s in outs],
        in_specs=specs,
        out_specs=[VMEM] * len(outs),
        scratch_shapes=scratch,
        name=name,
        compiler_params=pltpu.CompilerParams(vmem_limit_bytes=room * 2**20),
    )


def shift(value, axis, by):
    n = lax.axis_size(axis)
    return lax.ppermute(value, axis, [(i, (i + by) % n) for i in range(n)])


def spread_sum(value, axes):
    count = lax.axis_size(axes)
    copies = jnp.broadcast_to(value[None], (count, *value.shape))
    return jnp.sum(lax.all_to_all(copies, axes, 0, 0), axis=0)


FAR = ("z", "c")
NEAR = ("yl", "x", "yh")


def shards(jac_cam, jac_tex, residual, obs_slot, col_ids, block_pattern, damping):
    cam, tex = jac_cam[0, 0], jac_tex[0, 0]
    res, obs = residual[0], obs_slot[0, 0]
    damping = damping.reshape(1)

    *pieces, tex_part = call(
        local_kernel,
        "local",
        [(4 * PIECE, BLOCK)] * 4 + [(16, 24, BLOCK)],
        [HBM] * 6,
        LOCAL_SCRATCH,
        60,
    )(cam, tex, res, obs, col_ids, block_pattern)

    moved = [pieces[0]] + [shift(pieces[k], "x", k) for k in (1, 2, 3)]
    (own,) = call(add_kernel, "add", [(4 * PIECE, BLOCK)], [VMEM] * 4)(*moved)

    share = jnp.sum(lax.all_to_all(tex_part, FAR, 0, 0), axis=0)
    share = spread_sum(share, NEAR)
    share, own = lax.optimization_barrier((share, own))
    copies = jnp.broadcast_to(share[None], (16, *share.shape))
    tex_sums = lax.all_to_all(copies, FAR, 0, 0)
    parts = lax.all_to_all(own.reshape(4, PIECE, BLOCK), "yl", 0, 0)

    texture_factor, inverse, sol = call(
        panel_kernel, "panel", [(TEX_W, TEX_W), (TEX_W, TEX_W), (1, TEX_W)], [VMEM, SMEM], PANEL
    )(tex_sums, damping)
    reduced, gradient, coupling = call(
        last_kernel,
        "last",
        [(BLOCK, BLOCK), (1, BLOCK), (BLOCK, TEX_W)],
        [VMEM] * 3 + [SMEM],
    )(parts, inverse, sol, damping)
    return (reduced[None, None], gradient[None], coupling[None, None], texture_factor)


def solution(mesh):
    fine = Mesh(mesh.devices.reshape(4, 4, 2, 8, 2), ("yl", "x", "yh", "z", "c"))
    img, blk = ("yl", "x"), ("yh", "z", "c")
    return jax.shard_map(
        shards,
        mesh=fine,
        in_specs=(
            P(img, blk, None, None),
            P(img, blk, None, None),
            P(img, blk, None),
            P(img, blk, None),
            P(blk),
            P(),
            P(),
        ),
        out_specs=(
            P(blk, img, None, None),
            P(blk, img, None),
            P(blk, img, None, None),
            P(),
        ),
        check_vma=False,
    )
```

```python
import functools

import jax
import jax.numpy as jnp
from jax import lax
from jax.experimental import pallas as pl
from jax.experimental.pallas import tpu as pltpu
from jax.sharding import Mesh, PartitionSpec as P

BLOCK = 128
TEX_W = 256
ROWS = 1536
OBS = 192
PER = 8
SLOTS = 16
PIECE = 328
F32 = jnp.float32
VMEM = pl.BlockSpec(memory_space=pltpu.VMEM)
HBM = pl.BlockSpec(memory_space=pltpu.HBM)
SMEM = pl.BlockSpec(memory_space=pltpu.SMEM)


def col_dot(left, right):
    return lax.dot_general(left, right, (((0,), (0,)), ((), ())), preferred_element_type=F32)


def exact_dot(left, right, dims=((1,), (0,))):
    return lax.dot_general(
        left, right, (dims, ((), ())), precision=lax.Precision.HIGHEST, preferred_element_type=F32
    )


def iota(shape, dim):
    return lax.broadcasted_iota(jnp.int32, shape, dim)


def find_starts(obs_ref, starts):
    starts[SLOTS] = OBS

    def step(i, carry):
        j = OBS - 1 - i
        starts[obs_ref[j]] = j
        return carry

    lax.fori_loop(0, OBS, step, 0, unroll=8)


def fetch(pairs, sems):
    copies = []
    for src, dst in pairs:
        step = dst.shape[0] // 4 if dst.shape[0] == ROWS else dst.shape[0]
        for n in range(0, dst.shape[0], step):
            part = pl.ds(n, step)
            copies.append(pltpu.make_async_copy(src.at[part], dst.at[part], sems.at[len(copies)]))
    for copy in copies:
        copy.start()
    return copies


def tex_kernel(
    tex_any, res_any, obs_any, ids_any, pattern_any, out_ref,
    starts, tex_ref, res_ref, obs_ref, ids_ref, pattern_ref, sems,
):
    copies = fetch(
        (
            (obs_any, obs_ref),
            (ids_any, ids_ref),
            (pattern_any, pattern_ref),
            (res_any, res_ref),
            (tex_any, tex_ref),
        ),
        sems,
    )
    for copy in copies[:4]:
        copy.wait()
    find_starts(obs_ref, starts)
    for copy in copies[4:]:
        copy.wait()
    obs_index = iota((OBS, BLOCK), 0)
    masks = []
    for bit in range(2):
        keep = jnp.zeros((OBS, BLOCK), jnp.int32)
        for s in range(SLOTS):
            keep = jnp.where(obs_index >= starts[s], (pattern_ref[ids_ref[s]] >> bit) & 1, keep)
        rows = jnp.broadcast_to(keep.astype(F32)[:, None, :], (OBS, PER, BLOCK))
        masks.append(rows.reshape(ROWS, BLOCK).astype(jnp.bfloat16))
    masked = tex_ref[...] * jnp.concatenate(masks, axis=1)
    hess = col_dot(masked, masked)
    grad = jnp.dot(res_ref[...], masked, preferred_element_type=F32)
    h00, h10, h11 = hess[:BLOCK, :BLOCK], hess[BLOCK:, :BLOCK], hess[BLOCK:, BLOCK:]
    row, col = iota((BLOCK, BLOCK), 0), iota((BLOCK, BLOCK), 1)
    mixed = jnp.where(row >= col, h00, h11)
    diag = jnp.sum(jnp.where(row == col, h11, 0.0), axis=0, keepdims=True)
    out_ref[:, 8:, :] = jnp.zeros((32, 8, BLOCK), F32)
    out_ref[:16, :8, :] = mixed.reshape(16, 8, BLOCK)
    out_ref[16:, :8, :] = h10.reshape(16, 8, BLOCK)
    out_ref[0, 8:9, :] = grad[:, :BLOCK]
    out_ref[1, 8:9, :] = grad[:, BLOCK:]
    out_ref[2, 8:9, :] = diag


def packed(hess):
    row, lane = iota((64, BLOCK), 0), iota((64, BLOCK), 1)
    low, high = hess[64:, :], hess[:64, :]
    turned = pltpu.roll(high, 64, 1)
    pair = jnp.where((lane >= 64) & (row >= lane - 64), turned, low)
    return pair, jnp.sum(jnp.where(row == lane - 64, low, 0.0), axis=0, keepdims=True)


def cam_kernel(
    cam_any, tex_any, res_any, obs_any, ids_any, pattern_any, out0, out1, out2, out3,
    starts, cam_ref, tex_ref, res_ref, obs_ref, ids_ref, pattern_ref, sems,
):
    outs, my_x, my_yl = (out0, out1, out2, out3), lax.axis_index("x"), lax.axis_index("yl")
    copies = fetch(
        (
            (obs_any, obs_ref),
            (ids_any, ids_ref),
            (pattern_any, pattern_ref),
            (res_any, res_ref),
            (cam_any, cam_ref),
            (tex_any, tex_ref),
        ),
        sems,
    )
    for copy in copies[:4]:
        copy.wait()
    find_starts(obs_ref, starts)
    sub = iota((SLOTS, BLOCK), 0)
    first = jnp.zeros((SLOTS, BLOCK), jnp.int32)
    last = jnp.zeros((SLOTS, BLOCK), jnp.int32)
    for copy in copies[4:]:
        copy.wait()

    def bounds(k, j):
        slot = ((my_yl + j) & 3) * 4 + ((my_x + k) & 3)
        lo, hi = starts[slot] * PER, starts[slot + 1] * PER
        begin = pl.multiple_of(jnp.minimum((lo >> 4) << 4, ROWS - 256), 16)
        code = pattern_ref[ids_ref[slot]]
        return lo, hi, begin, (code & 1) == 1, (code >> 1) == 1

    def part(begin, lo, hi, count):
        cam = cam_ref[pl.ds(begin, count), :]
        both = jnp.concatenate([cam, tex_ref[pl.ds(begin, count), :]], axis=1)
        where = iota((count, BLOCK), 0) + begin
        keep = ((where >= lo) & (where < hi)).astype(F32).astype(jnp.bfloat16)
        return col_dot(cam * keep, both)

    zero = jnp.zeros((BLOCK, BLOCK), F32)
    for k in range(4):
        for j in range(4):
            out, base = outs[k], j * PIECE
            lo, hi, begin, keep0, keep1 = bounds(k, j)
            first = jnp.where(sub == k * 4 + j, lo, first)
            last = jnp.where(sub == k * 4 + j, hi, last)
            sums = part(begin, lo, hi, 256)
            pair, diag = packed(sums[:, :BLOCK])
            out[base : base + 128, :] = jnp.where(keep0, sums[:, BLOCK : 2 * BLOCK], zero)
            out[base + 128 : base + 256, :] = jnp.where(keep1, sums[:, 2 * BLOCK :], zero)
            out[base + 256 : base + 320, :] = pair
            out[base + 320 : base + 328, :] = jnp.broadcast_to(diag, (8, BLOCK))

    lane = iota((SLOTS, ROWS), 1)
    first = jnp.tile(first, (1, ROWS // BLOCK))
    last = jnp.tile(last, (1, ROWS // BLOCK))
    res = jnp.broadcast_to(res_ref[...].astype(F32), (SLOTS, ROWS))
    spread = jnp.where((lane >= first) & (lane < last), res, 0.0).astype(jnp.bfloat16)
    grad = jnp.dot(spread, cam_ref[...], preferred_element_type=F32)
    for i in range(SLOTS):
        base = (i % 4) * PIECE
        outs[i // 4][base + 320 : base + 321, :] = grad[i : i + 1, :]

    for k in range(4):
        for j in range(4):
            out, base = outs[k], j * PIECE
            lo, hi, begin, keep0, keep1 = bounds(k, j)

            @pl.when(hi > begin + 256)
            def _():
                second = pl.multiple_of(jnp.minimum(begin + 256, ROWS - 48), 16)
                sums = part(second, begin + 256, hi, 48)
                pair, diag = packed(sums[:, :BLOCK])
                out[base : base + 128, :] += jnp.where(keep0, sums[:, BLOCK : 2 * BLOCK], zero)
                out[base + 128 : base + 256, :] += jnp.where(keep1, sums[:, 2 * BLOCK :], zero)
                out[base + 256 : base + 320, :] += pair
                out[base + 321 : base + 322, :] += diag


def add_kernel(a_ref, b_ref, c_ref, d_ref, *outs):
    for j in range(4):
        rows = slice(j * PIECE, (j + 1) * PIECE)
        outs[j][...] = (a_ref[rows, :] + b_ref[rows, :]) + (c_ref[rows, :] + d_ref[rows, :])


def split3(value):
    high = value.astype(jnp.bfloat16)
    return high, (value - high.astype(F32)).astype(jnp.bfloat16)


def near_dot(left, right, dims=((1,), (0,))):
    (lk,), (rk,) = dims
    lh, ll = split3(left)
    rh, rl = split3(right)
    return lax.dot_general(
        jnp.concatenate([lh, lh, ll], axis=lk),
        jnp.concatenate([rh, rl, rh], axis=rk),
        (dims, ((), ())),
        preferred_element_type=F32,
    )


def lanes(value, k):
    return jnp.broadcast_to(value[:, k : k + 1], (8, BLOCK))


def subs(value, j):
    return jnp.broadcast_to(value[j : j + 1, :], (8, BLOCK))


def factor(ab, upper, block):
    row, col = iota((BLOCK, BLOCK), 0), iota((BLOCK, BLOCK), 1)
    sub = iota((8, BLOCK), 0)
    ab[:, :BLOCK] = block
    ab[:, BLOCK:] = (row == col).astype(F32)
    cur = [block[:8], ab[:8, BLOCK:]]
    for b in range(16):
        more = b < 15
        heads = [lanes(cur[0], 8 * b + k) for k in range(8)]
        if more:
            rows = slice(8 * (b + 1), 8 * (b + 2))
            below = [ab[rows, :BLOCK], ab[rows, BLOCK:]]
            tails = [lanes(below[0], 8 * b + k) for k in range(8)]
        for j in range(8):
            scale = lax.rsqrt(subs(heads[j], j))
            head = jnp.where(sub > j, heads[j] * scale, 0.0)
            for k in range(j + 1, 8):
                pick = subs(heads[k], j) * scale
                heads[k] = heads[k] - head * pick
                if more:
                    if k == j + 1:
                        tail = tails[j] * scale
                    tails[k] = tails[k] - tail * pick
            if more and j == 7:
                tail = tails[j] * scale
            for part in range(2):
                pivot = subs(cur[part], j) * scale
                cur[part] = jnp.where(sub == j, pivot, cur[part] - head * pivot)
                if more:
                    below[part] = below[part] - tail * pivot
        done = jnp.concatenate(cur, axis=1)
        upper[8 * b : 8 * b + 8, :] = done
        if b < 14:
            high, low = split3(done)
            update = col_dot(
                jnp.concatenate([high[:, :BLOCK], high[:, :BLOCK], low[:, :BLOCK]], axis=0),
                jnp.concatenate([high, low, high], axis=0),
            )
            ab[8 * (b + 2) :, :] -= update[8 * (b + 2) :, :]
        if more:
            cur = below
    return jnp.where(row >= col, upper[:, :BLOCK].T, 0.0), upper[:, BLOCK:]


def panel_kernel(sums_ref, damping_ref, factor_ref, inv_ref, sol_ref, ab, upper):
    damping = damping_ref[0]
    sums = sums_ref[...]
    both = sums[:, :8, :].reshape(TEX_W, BLOCK)
    mixed, h10 = both[:BLOCK], both[BLOCK:]
    g0, g1, diag = sums[0, 8:9, :], sums[1, 8:9, :], sums[2, 8:9, :]
    row, col = iota((BLOCK, BLOCK), 0), iota((BLOCK, BLOCK), 1)
    flipped = mixed.T
    h00 = jnp.where(row >= col, mixed, flipped)
    h11 = jnp.where(row < col, mixed, jnp.where(row == col, diag, flipped))
    h00 = jnp.where(row == col, h00 + damping * h00, h00)
    h11 = jnp.where(row == col, h11 + damping * h11, h11)
    across = ((1,), (1,))
    l00, w00 = factor(ab, upper, h00)
    l10 = near_dot(h10, w00, across)
    y0 = near_dot(g0, w00, across)
    zero = jnp.zeros((BLOCK, BLOCK), F32)
    factor_ref[:BLOCK, :BLOCK] = l00
    factor_ref[:BLOCK, BLOCK:] = zero
    factor_ref[BLOCK:, :BLOCK] = l10
    inv_ref[:BLOCK, :BLOCK] = w00
    inv_ref[:BLOCK, BLOCK:] = zero
    lw = near_dot(l10, w00)
    l11, w11 = factor(ab, upper, h11 - near_dot(l10, l10, across))
    factor_ref[BLOCK:, BLOCK:] = l11
    inv_ref[BLOCK:, :BLOCK] = -near_dot(w11, lw)
    inv_ref[BLOCK:, BLOCK:] = w11
    sol_ref[:, :BLOCK] = y0
    sol_ref[:, BLOCK:] = near_dot(g1 - near_dot(y0, l10, across), w11, across)


def last_kernel(a_ref, b_ref, c_ref, d_ref, inv_ref, sol_ref, damping_ref, red_ref, grad_ref, coup_ref):
    damping = damping_ref[0]
    total = (a_ref[...] + b_ref[...]) + (c_ref[...] + d_ref[...])
    cross = jnp.concatenate([total[:128], total[128:256]], axis=1)
    pair, grad, diag = total[256:320], total[320:321], total[321:322]
    row, col = iota((BLOCK, BLOCK), 0), iota((BLOCK, BLOCK), 1)
    row64, lane64 = iota((64, BLOCK), 0), iota((64, BLOCK), 1)
    turned = pltpu.roll(pair, 64, 1)
    top = jnp.where(lane64 < 64, turned, 0.0)
    square = jnp.concatenate([top, pair], axis=0)
    other = square.T
    lower = jnp.where((row >= 64) & (col >= 64), other, square)
    lower = jnp.where(row > col, lower, 0.0)
    main = jnp.where(row == col, jnp.where(row < 64, square, diag), 0.0)
    hess = lower + lower.T + main + damping * main
    coupling = exact_dot(cross, inv_ref[...], ((1,), (1,)))
    coup_ref[...] = coupling
    red_ref[...] = hess - exact_dot(coupling, coupling, ((1,), (1,)))
    grad_ref[...] = grad - exact_dot(sol_ref[...], coupling, ((1,), (1,)))


SMALL_SCRATCH = [
    pltpu.VMEM((ROWS, TEX_W), jnp.bfloat16),
    pltpu.VMEM((1, ROWS), jnp.bfloat16),
    pltpu.SMEM((OBS,), jnp.int32),
    pltpu.SMEM((SLOTS,), jnp.int32),
    pltpu.SMEM((512,), jnp.int32),
    pltpu.SemaphoreType.DMA((12,)),
]
TEX_SCRATCH = [pltpu.SMEM((SLOTS + 1,), jnp.int32), *SMALL_SCRATCH]
CAM_SCRATCH = [TEX_SCRATCH[0], pltpu.VMEM((ROWS, BLOCK), jnp.bfloat16), *SMALL_SCRATCH]
PANEL = [pltpu.VMEM((BLOCK, TEX_W), F32), pltpu.VMEM((BLOCK, TEX_W), F32)]


def call(kernel, name, outs, specs, scratch=(), room=24):
    return pl.pallas_call(
        kernel,
        out_shape=[jax.ShapeDtypeStruct(s, F32) for s in outs],
        in_specs=specs,
        out_specs=[VMEM] * len(outs),
        scratch_shapes=scratch,
        name=name,
        compiler_params=pltpu.CompilerParams(vmem_limit_bytes=room * 2**20),
    )


def shift(value, axis, by):
    n = lax.axis_size(axis)
    return lax.ppermute(value, axis, [(i, (i + by) % n) for i in range(n)])


def spread_sum(value, axes):
    count = lax.axis_size(axes)
    copies = jnp.broadcast_to(value[None], (count, *value.shape))
    return jnp.sum(lax.all_to_all(copies, axes, 0, 0), axis=0)


FAR = ("x", "z")
NEAR = ("yl", "yh", "c")


def shards(jac_cam, jac_tex, residual, obs_slot, col_ids, block_pattern, damping):
    cam, tex = jac_cam[0, 0], jac_tex[0, 0]
    res, obs = residual[0], obs_slot[0, 0]
    damping = damping.reshape(1)

    (tex_part,) = call(tex_kernel, "tex", [(32, 16, BLOCK)], [HBM] * 5, TEX_SCRATCH, 60)(
        tex, res, obs, col_ids, block_pattern
    )
    pieces = call(cam_kernel, "cam", [(4 * PIECE, BLOCK)] * 4, [HBM] * 6, CAM_SCRATCH, 60)(
        cam, tex, res, obs, col_ids, block_pattern
    )
    moved = [pieces[0]] + [shift(pieces[k], "x", k) for k in (1, 2, 3)]
    pieces = call(add_kernel, "add", [(PIECE, BLOCK)] * 4, [VMEM] * 4)(*moved)
    moved = [pieces[0]] + [shift(pieces[j], "yl", j) for j in (1, 2, 3)]

    share = jnp.sum(lax.all_to_all(tex_part, FAR, 0, 0), axis=0)
    share = spread_sum(share, NEAR)
    copies = jnp.broadcast_to(share[None], (32, *share.shape))
    tex_sums = lax.all_to_all(copies, FAR, 0, 0)

    texture_factor, inverse, sol = call(
        panel_kernel, "panel", [(TEX_W, TEX_W), (TEX_W, TEX_W), (1, TEX_W)], [VMEM, SMEM], PANEL
    )(tex_sums, damping)
    reduced, gradient, coupling = call(
        last_kernel,
        "last",
        [(BLOCK, BLOCK), (1, BLOCK), (BLOCK, TEX_W)],
        [VMEM] * 6 + [SMEM],
    )(*moved, inverse, sol, damping)
    return (reduced[None, None], gradient[None], coupling[None, None], texture_factor)


def solution(mesh):
    fine = Mesh(mesh.devices.reshape(4, 4, 2, 8, 2), ("yl", "x", "yh", "z", "c"))
    img, blk = ("yl", "x"), ("yh", "z", "c")
    return jax.shard_map(
        shards,
        mesh=fine,
        in_specs=(
            P(img, blk, None, None),
            P(img, blk, None, None),
            P(img, blk, None),
            P(img, blk, None),
            P(blk),
            P(),
            P(),
        ),
        out_specs=(
            P(blk, img, None, None),
            P(blk, img, None),
            P(blk, img, None, None),
            P(),
        ),
        check_vma=False,
    )
```

```python
import functools

import jax
import jax.numpy as jnp
from jax import lax
from jax.experimental import pallas as pl
from jax.experimental.pallas import tpu as pltpu
from jax.sharding import Mesh, PartitionSpec as P

BLOCK = 128
TEX_W = 256
ROWS = 1536
OBS = 192
PER = 8
SLOTS = 16
FAR_N = 16
SHARE = TEX_W // FAR_N
PIECE = 328
F32 = jnp.float32
VMEM = pl.BlockSpec(memory_space=pltpu.VMEM)
HBM = pl.BlockSpec(memory_space=pltpu.HBM)
SMEM = pl.BlockSpec(memory_space=pltpu.SMEM)


def col_dot(left, right):
    return lax.dot_general(left, right, (((0,), (0,)), ((), ())), preferred_element_type=F32)


def exact_dot(left, right, dims=((1,), (0,))):
    return lax.dot_general(
        left, right, (dims, ((), ())), precision=lax.Precision.HIGHEST, preferred_element_type=F32
    )


def iota(shape, dim):
    return lax.broadcasted_iota(jnp.int32, shape, dim)


def find_starts(obs_ref, starts):
    starts[SLOTS] = OBS

    def step(i, carry):
        j = OBS - 1 - i
        starts[obs_ref[j]] = j
        return carry

    lax.fori_loop(0, OBS, step, 0, unroll=8)


def fetch(pairs, sems):
    copies = []
    for src, dst in pairs:
        step = dst.shape[0] // 4 if dst.shape[0] == ROWS else dst.shape[0]
        for n in range(0, dst.shape[0], step):
            part = pl.ds(n, step)
            copies.append(pltpu.make_async_copy(src.at[part], dst.at[part], sems.at[len(copies)]))
    for copy in copies:
        copy.start()
    return copies


def tex_sums(tex_ref, res_ref, ids_ref, pattern_ref, starts, out_ref):
    obs_index = iota((OBS, BLOCK), 0)
    masks = []
    for bit in range(2):
        keep = jnp.zeros((OBS, BLOCK), jnp.int32)
        for s in range(SLOTS):
            keep = jnp.where(obs_index >= starts[s], (pattern_ref[ids_ref[s]] >> bit) & 1, keep)
        rows = jnp.broadcast_to(keep.astype(F32)[:, None, :], (OBS, PER, BLOCK))
        masks.append(rows.reshape(ROWS, BLOCK).astype(jnp.bfloat16))
    masked = tex_ref[...] * jnp.concatenate(masks, axis=1)
    hess = col_dot(masked, masked)
    grad = jnp.dot(res_ref[...], masked, preferred_element_type=F32)
    h00, h10, h11 = hess[:BLOCK, :BLOCK], hess[BLOCK:, :BLOCK], hess[BLOCK:, BLOCK:]
    row, col = iota((BLOCK, BLOCK), 0), iota((BLOCK, BLOCK), 1)
    mixed = jnp.where(row >= col, h00, h11)
    diag = jnp.sum(jnp.where(row == col, h11, 0.0), axis=0, keepdims=True)
    half = FAR_N // 2
    out_ref[:, SHARE:, :] = jnp.zeros((FAR_N, 1, BLOCK), F32)
    out_ref[:half, :SHARE, :] = mixed.reshape(half, SHARE, BLOCK)
    out_ref[half:, :SHARE, :] = h10.reshape(half, SHARE, BLOCK)
    out_ref[0, SHARE:, :] = grad[:, :BLOCK]
    out_ref[1, SHARE:, :] = grad[:, BLOCK:]
    out_ref[2, SHARE:, :] = diag


def packed(hess):
    row, lane = iota((64, BLOCK), 0), iota((64, BLOCK), 1)
    low, high = hess[64:, :], hess[:64, :]
    turned = pltpu.roll(high, 64, 1)
    pair = jnp.where((lane >= 64) & (row >= lane - 64), turned, low)
    return pair, jnp.sum(jnp.where(row == lane - 64, low, 0.0), axis=0, keepdims=True)


def local_kernel(
    cam_any, tex_any, res_any, obs_any, ids_any, pattern_any, out0, out1, out2, out3, tex_out,
    starts, cam_ref, tex_ref, res_ref, obs_ref, ids_ref, pattern_ref, sems,
):
    outs, my_x, my_yl = (out0, out1, out2, out3), lax.axis_index("x"), lax.axis_index("yl")
    copies = fetch(
        (
            (obs_any, obs_ref),
            (ids_any, ids_ref),
            (pattern_any, pattern_ref),
            (res_any, res_ref),
            (cam_any, cam_ref),
            (tex_any, tex_ref),
        ),
        sems,
    )
    for copy in copies[:4]:
        copy.wait()
    find_starts(obs_ref, starts)
    sub = iota((SLOTS, BLOCK), 0)
    first = jnp.zeros((SLOTS, BLOCK), jnp.int32)
    last = jnp.zeros((SLOTS, BLOCK), jnp.int32)
    for copy in copies[4:]:
        copy.wait()
    tex_sums(tex_ref, res_ref, ids_ref, pattern_ref, starts, tex_out)

    def bounds(k, j):
        slot = ((my_yl + j) & 3) * 4 + ((my_x + k) & 3)
        lo, hi = starts[slot] * PER, starts[slot + 1] * PER
        begin = pl.multiple_of(jnp.minimum((lo >> 4) << 4, ROWS - 256), 16)
        code = pattern_ref[ids_ref[slot]]
        return lo, hi, begin, (code & 1) == 1, (code >> 1) == 1

    def part(begin, lo, hi, count):
        cam = cam_ref[pl.ds(begin, count), :]
        both = jnp.concatenate([cam, tex_ref[pl.ds(begin, count), :]], axis=1)
        where = iota((count, BLOCK), 0) + begin
        keep = ((where >= lo) & (where < hi)).astype(F32).astype(jnp.bfloat16)
        return col_dot(cam * keep, both)

    zero = jnp.zeros((BLOCK, BLOCK), F32)
    for k in range(4):
        for j in range(4):
            out, base = outs[k], j * PIECE
            lo, hi, begin, keep0, keep1 = bounds(k, j)
            first = jnp.where(sub == k * 4 + j, lo, first)
            last = jnp.where(sub == k * 4 + j, hi, last)
            sums = part(begin, lo, hi, 256)
            pair, diag = packed(sums[:, :BLOCK])
            out[base : base + 128, :] = jnp.where(keep0, sums[:, BLOCK : 2 * BLOCK], zero)
            out[base + 128 : base + 256, :] = jnp.where(keep1, sums[:, 2 * BLOCK :], zero)
            out[base + 256 : base + 320, :] = pair
            out[base + 320 : base + 328, :] = jnp.broadcast_to(diag, (8, BLOCK))

    lane = iota((SLOTS, ROWS), 1)
    first = jnp.tile(first, (1, ROWS // BLOCK))
    last = jnp.tile(last, (1, ROWS // BLOCK))
    res = jnp.broadcast_to(res_ref[...].astype(F32), (SLOTS, ROWS))
    spread = jnp.where((lane >= first) & (lane < last), res, 0.0).astype(jnp.bfloat16)
    grad = jnp.dot(spread, cam_ref[...], preferred_element_type=F32)
    for i in range(SLOTS):
        base = (i % 4) * PIECE
        outs[i // 4][base + 320 : base + 321, :] = grad[i : i + 1, :]

    for k in range(4):
        for j in range(4):
            out, base = outs[k], j * PIECE
            lo, hi, begin, keep0, keep1 = bounds(k, j)

            @pl.when(hi > begin + 256)
            def _():
                second = pl.multiple_of(jnp.minimum(begin + 256, ROWS - 48), 16)
                sums = part(second, begin + 256, hi, 48)
                pair, diag = packed(sums[:, :BLOCK])
                out[base : base + 128, :] += jnp.where(keep0, sums[:, BLOCK : 2 * BLOCK], zero)
                out[base + 128 : base + 256, :] += jnp.where(keep1, sums[:, 2 * BLOCK :], zero)
                out[base + 256 : base + 320, :] += pair
                out[base + 321 : base + 322, :] += diag


def near_kernel(a_ref, b_ref, c_ref, out_ref):
    out_ref[...] = (a_ref[...] + b_ref[...]) + c_ref[...]


def add_kernel(a_ref, b_ref, *outs):
    for j in range(4):
        rows = slice(j * PIECE, (j + 1) * PIECE)
        outs[j][...] = a_ref[rows, :] + b_ref[rows, :]


def split3(value):
    high = value.astype(jnp.bfloat16)
    return high, (value - high.astype(F32)).astype(jnp.bfloat16)


def near_dot(left, right, dims=((1,), (0,))):
    (lk,), (rk,) = dims
    lh, ll = split3(left)
    rh, rl = split3(right)
    return lax.dot_general(
        jnp.concatenate([lh, lh, ll], axis=lk),
        jnp.concatenate([rh, rl, rh], axis=rk),
        (dims, ((), ())),
        preferred_element_type=F32,
    )


def lanes(value, k):
    return jnp.broadcast_to(value[:, k : k + 1], (8, BLOCK))


def subs(value, j):
    return jnp.broadcast_to(value[j : j + 1, :], (8, BLOCK))


def factor(ab, upper, block):
    row, col = iota((BLOCK, BLOCK), 0), iota((BLOCK, BLOCK), 1)
    sub = iota((8, BLOCK), 0)
    ab[:, :BLOCK] = block
    ab[:, BLOCK:] = (row == col).astype(F32)
    cur = [block[:8], ab[:8, BLOCK:]]
    for b in range(16):
        more = b < 15
        heads = [lanes(cur[0], 8 * b + k) for k in range(8)]
        if more:
            rows = slice(8 * (b + 1), 8 * (b + 2))
            below = [ab[rows, :BLOCK], ab[rows, BLOCK:]]
            tails = [lanes(below[0], 8 * b + k) for k in range(8)]
        for j in range(8):
            scale = lax.rsqrt(subs(heads[j], j))
            head = jnp.where(sub > j, heads[j] * scale, 0.0)
            for k in range(j + 1, 8):
                pick = subs(heads[k], j) * scale
                heads[k] = heads[k] - head * pick
                if more:
                    if k == j + 1:
                        tail = tails[j] * scale
                    tails[k] = tails[k] - tail * pick
            if more and j == 7:
                tail = tails[j] * scale
            for part in range(2):
                pivot = subs(cur[part], j) * scale
                cur[part] = jnp.where(sub == j, pivot, cur[part] - head * pivot)
                if more:
                    below[part] = below[part] - tail * pivot
        done = jnp.concatenate(cur, axis=1)
        upper[8 * b : 8 * b + 8, :] = done
        if b < 14:
            high, low = split3(done)
            update = col_dot(
                jnp.concatenate([high[:, :BLOCK], high[:, :BLOCK], low[:, :BLOCK]], axis=0),
                jnp.concatenate([high, low, high], axis=0),
            )
            ab[8 * (b + 2) :, :] -= update[8 * (b + 2) :, :]
        if more:
            cur = below
    return jnp.where(row >= col, upper[:, :BLOCK].T, 0.0), upper[:, BLOCK:]


def panel_kernel(sums_ref, damping_ref, factor_ref, inv_ref, sol_ref, ab, upper):
    damping = damping_ref[0]
    sums = sums_ref[...]
    both = sums[:, :SHARE, :].reshape(TEX_W, BLOCK)
    mixed, h10 = both[:BLOCK], both[BLOCK:]
    g0, g1, diag = sums[0, SHARE:, :], sums[1, SHARE:, :], sums[2, SHARE:, :]
    row, col = iota((BLOCK, BLOCK), 0), iota((BLOCK, BLOCK), 1)
    flipped = mixed.T
    h00 = jnp.where(row >= col, mixed, flipped)
    h11 = jnp.where(row < col, mixed, jnp.where(row == col, diag, flipped))
    h00 = jnp.where(row == col, h00 + damping * h00, h00)
    h11 = jnp.where(row == col, h11 + damping * h11, h11)
    across = ((1,), (1,))
    l00, w00 = factor(ab, upper, h00)
    l10 = near_dot(h10, w00, across)
    y0 = near_dot(g0, w00, across)
    zero = jnp.zeros((BLOCK, BLOCK), F32)
    factor_ref[:BLOCK, :BLOCK] = l00
    factor_ref[:BLOCK, BLOCK:] = zero
    factor_ref[BLOCK:, :BLOCK] = l10
    inv_ref[:BLOCK, :BLOCK] = w00
    inv_ref[:BLOCK, BLOCK:] = zero
    lw = near_dot(l10, w00)
    l11, w11 = factor(ab, upper, h11 - near_dot(l10, l10, across))
    factor_ref[BLOCK:, BLOCK:] = l11
    inv_ref[BLOCK:, :BLOCK] = -near_dot(w11, lw)
    inv_ref[BLOCK:, BLOCK:] = w11
    sol_ref[:, :BLOCK] = y0
    sol_ref[:, BLOCK:] = near_dot(g1 - near_dot(y0, l10, across), w11, across)


def last_kernel(a_ref, b_ref, c_ref, d_ref, inv_ref, sol_ref, damping_ref, red_ref, grad_ref, coup_ref):
    damping = damping_ref[0]
    total = (a_ref[...] + b_ref[...]) + (c_ref[...] + d_ref[...])
    cross = jnp.concatenate([total[:128], total[128:256]], axis=1)
    pair, grad, diag = total[256:320], total[320:321], total[321:322]
    row, col = iota((BLOCK, BLOCK), 0), iota((BLOCK, BLOCK), 1)
    row64, lane64 = iota((64, BLOCK), 0), iota((64, BLOCK), 1)
    turned = pltpu.roll(pair, 64, 1)
    top = jnp.where(lane64 < 64, turned, 0.0)
    square = jnp.concatenate([top, pair], axis=0)
    other = square.T
    lower = jnp.where((row >= 64) & (col >= 64), other, square)
    lower = jnp.where(row > col, lower, 0.0)
    main = jnp.where(row == col, jnp.where(row < 64, square, diag), 0.0)
    hess = lower + lower.T + main + damping * main
    coupling = exact_dot(cross, inv_ref[...], ((1,), (1,)))
    coup_ref[...] = coupling
    red_ref[...] = hess - exact_dot(coupling, coupling, ((1,), (1,)))
    grad_ref[...] = grad - exact_dot(sol_ref[...], coupling, ((1,), (1,)))


LOCAL_SCRATCH = [
    pltpu.SMEM((SLOTS + 1,), jnp.int32),
    pltpu.VMEM((ROWS, BLOCK), jnp.bfloat16),
    pltpu.VMEM((ROWS, TEX_W), jnp.bfloat16),
    pltpu.VMEM((1, ROWS), jnp.bfloat16),
    pltpu.SMEM((OBS,), jnp.int32),
    pltpu.SMEM((SLOTS,), jnp.int32),
    pltpu.SMEM((512,), jnp.int32),
    pltpu.SemaphoreType.DMA((12,)),
]
COST = {
    name: pl.CostEstimate(flops=flops, bytes_accessed=0, transcendentals=0)
    for name, flops in {"near": 6_000_000_000, "add": 1_000_000_000}.items()
}
PANEL = [pltpu.VMEM((BLOCK, TEX_W), F32), pltpu.VMEM((BLOCK, TEX_W), F32)]


def call(kernel, name, outs, specs, scratch=(), room=24):
    return pl.pallas_call(
        kernel,
        cost_estimate=COST.get(name),
        out_shape=[jax.ShapeDtypeStruct(s, F32) for s in outs],
        in_specs=specs,
        out_specs=[VMEM] * len(outs),
        scratch_shapes=scratch,
        name=name,
        compiler_params=pltpu.CompilerParams(vmem_limit_bytes=room * 2**20),
    )


def shift(value, axis, by):
    n = lax.axis_size(axis)
    return lax.ppermute(value, axis, [(i, (i + by) % n) for i in range(n)])


def spread_sum(value, axes):
    count = lax.axis_size(axes)
    copies = jnp.broadcast_to(value[None], (count, *value.shape))
    return jnp.sum(lax.all_to_all(copies, axes, 0, 0), axis=0)


FAR = ("z", "c")
NEAR = ("yl", "x", "yh")


def shards(jac_cam, jac_tex, residual, obs_slot, col_ids, block_pattern, damping):
    cam, tex = jac_cam[0, 0], jac_tex[0, 0]
    res, obs = residual[0], obs_slot[0, 0]
    damping = damping.reshape(1)

    *pieces, tex_part = call(
        local_kernel,
        "local",
        [(4 * PIECE, BLOCK)] * 4 + [(FAR_N, SHARE + 1, BLOCK)],
        [HBM] * 6,
        LOCAL_SCRATCH,
        60,
    )(cam, tex, res, obs, col_ids, block_pattern)
    beside = [pieces[0]] + [shift(pieces[k], "x", k) for k in (1, 3)]
    across = shift(pieces[2], "x", 2)
    (beside,) = call(near_kernel, "near", [(4 * PIECE, BLOCK)], [VMEM] * 3)(*beside)
    pieces = call(add_kernel, "add", [(PIECE, BLOCK)] * 4, [VMEM] * 2)(beside, across)
    moved = [pieces[0]] + [shift(pieces[j], "yl", j) for j in (1, 2, 3)]

    share = jnp.sum(lax.all_to_all(tex_part, FAR, 0, 0), axis=0)
    share = spread_sum(share, NEAR)
    copies = jnp.broadcast_to(share[None], (FAR_N, *share.shape))
    tex_sums = lax.all_to_all(copies, FAR, 0, 0)

    texture_factor, inverse, sol = call(
        panel_kernel, "panel", [(TEX_W, TEX_W), (TEX_W, TEX_W), (1, TEX_W)], [VMEM, SMEM], PANEL
    )(tex_sums, damping)
    reduced, gradient, coupling = call(
        last_kernel,
        "last",
        [(BLOCK, BLOCK), (1, BLOCK), (BLOCK, TEX_W)],
        [VMEM] * 6 + [SMEM],
    )(*moved, inverse, sol, damping)
    return (reduced[None, None], gradient[None], coupling[None, None], texture_factor)


def solution(mesh):
    fine = Mesh(mesh.devices.reshape(4, 4, 2, 8, 2), ("yl", "x", "yh", "z", "c"))
    img, blk = ("yl", "x"), ("yh", "z", "c")
    return jax.shard_map(
        shards,
        mesh=fine,
        in_specs=(
            P(img, blk, None, None),
            P(img, blk, None, None),
            P(img, blk, None),
            P(img, blk, None),
            P(blk),
            P(),
            P(),
        ),
        out_specs=(
            P(blk, img, None, None),
            P(blk, img, None),
            P(blk, img, None, None),
            P(),
        ),
        check_vma=False,
    )
```

```python
import functools

import jax
import jax.numpy as jnp
from jax import lax
from jax.experimental import pallas as pl
from jax.experimental.pallas import tpu as pltpu
from jax.sharding import Mesh, PartitionSpec as P

BLOCK = 128
TEX_W = 256
ROWS = 1536
OBS = 192
PER = 8
SLOTS = 16
FAR_N = 32
SHARE = TEX_W // FAR_N
PIECE = 328
F32 = jnp.float32
VMEM = pl.BlockSpec(memory_space=pltpu.VMEM)
HBM = pl.BlockSpec(memory_space=pltpu.HBM)
SMEM = pl.BlockSpec(memory_space=pltpu.SMEM)


def col_dot(left, right):
    return lax.dot_general(left, right, (((0,), (0,)), ((), ())), preferred_element_type=F32)


def exact_dot(left, right, dims=((1,), (0,))):
    return lax.dot_general(
        left, right, (dims, ((), ())), precision=lax.Precision.HIGHEST, preferred_element_type=F32
    )


def iota(shape, dim):
    return lax.broadcasted_iota(jnp.int32, shape, dim)


def find_starts(obs_ref, starts):
    starts[SLOTS] = OBS

    def step(i, carry):
        j = OBS - 1 - i
        starts[obs_ref[j]] = j
        return carry

    lax.fori_loop(0, OBS, step, 0, unroll=8)


def fetch(pairs, sems):
    copies = []
    for src, dst in pairs:
        step = dst.shape[0] // 4 if dst.shape[0] == ROWS else dst.shape[0]
        for n in range(0, dst.shape[0], step):
            part = pl.ds(n, step)
            copies.append(pltpu.make_async_copy(src.at[part], dst.at[part], sems.at[len(copies)]))
    for copy in copies:
        copy.start()
    return copies


def tex_sums(tex_ref, res_ref, ids_ref, pattern_ref, starts, out_ref):
    obs_index = iota((OBS, BLOCK), 0)
    masks = []
    for bit in range(2):
        keep = jnp.zeros((OBS, BLOCK), jnp.int32)
        for s in range(SLOTS):
            keep = jnp.where(obs_index >= starts[s], (pattern_ref[ids_ref[s]] >> bit) & 1, keep)
        rows = jnp.broadcast_to(keep.astype(F32)[:, None, :], (OBS, PER, BLOCK))
        masks.append(rows.reshape(ROWS, BLOCK).astype(jnp.bfloat16))
    masked = tex_ref[...] * jnp.concatenate(masks, axis=1)
    hess = col_dot(masked, masked)
    grad = jnp.dot(res_ref[...], masked, preferred_element_type=F32)
    h00, h10, h11 = hess[:BLOCK, :BLOCK], hess[BLOCK:, :BLOCK], hess[BLOCK:, BLOCK:]
    row, col = iota((BLOCK, BLOCK), 0), iota((BLOCK, BLOCK), 1)
    mixed = jnp.where(row >= col, h00, h11)
    diag = jnp.sum(jnp.where(row == col, h11, 0.0), axis=0, keepdims=True)
    half = FAR_N // 2
    out_ref[:, SHARE:, :] = jnp.zeros((FAR_N, SHARE, BLOCK), F32)
    out_ref[:half, :SHARE, :] = mixed.reshape(half, SHARE, BLOCK)
    out_ref[half:, :SHARE, :] = h10.reshape(half, SHARE, BLOCK)
    out_ref[0, SHARE : SHARE + 1, :] = grad[:, :BLOCK]
    out_ref[1, SHARE : SHARE + 1, :] = grad[:, BLOCK:]
    out_ref[2, SHARE : SHARE + 1, :] = diag


def packed(hess):
    row, lane = iota((64, BLOCK), 0), iota((64, BLOCK), 1)
    low, high = hess[64:, :], hess[:64, :]
    turned = pltpu.roll(high, 64, 1)
    pair = jnp.where((lane >= 64) & (row >= lane - 64), turned, low)
    return pair, jnp.sum(jnp.where(row == lane - 64, low, 0.0), axis=0, keepdims=True)


def local_kernel(
    cam_any, tex_any, res_any, obs_any, ids_any, pattern_any, out0, out1, out2, out3, tex_out,
    starts, cam_ref, tex_ref, res_ref, obs_ref, ids_ref, pattern_ref, sems,
):
    outs, my_x, my_yl = (out0, out1, out2, out3), lax.axis_index("x"), lax.axis_index("yl")
    copies = fetch(
        (
            (obs_any, obs_ref),
            (ids_any, ids_ref),
            (pattern_any, pattern_ref),
            (res_any, res_ref),
            (cam_any, cam_ref),
            (tex_any, tex_ref),
        ),
        sems,
    )
    for copy in copies[:4]:
        copy.wait()
    find_starts(obs_ref, starts)
    sub = iota((SLOTS, BLOCK), 0)
    first = jnp.zeros((SLOTS, BLOCK), jnp.int32)
    last = jnp.zeros((SLOTS, BLOCK), jnp.int32)
    for copy in copies[4:]:
        copy.wait()
    tex_sums(tex_ref, res_ref, ids_ref, pattern_ref, starts, tex_out)

    def bounds(k, j):
        slot = ((my_yl + j) & 3) * 4 + ((my_x + k) & 3)
        lo, hi = starts[slot] * PER, starts[slot + 1] * PER
        begin = pl.multiple_of(jnp.minimum((lo >> 4) << 4, ROWS - 256), 16)
        code = pattern_ref[ids_ref[slot]]
        return lo, hi, begin, (code & 1) == 1, (code >> 1) == 1

    def part(begin, lo, hi, count):
        cam = cam_ref[pl.ds(begin, count), :]
        both = jnp.concatenate([cam, tex_ref[pl.ds(begin, count), :]], axis=1)
        where = iota((count, BLOCK), 0) + begin
        keep = ((where >= lo) & (where < hi)).astype(F32).astype(jnp.bfloat16)
        return col_dot(cam * keep, both)

    zero = jnp.zeros((BLOCK, BLOCK), F32)
    for k in range(4):
        for j in range(4):
            out, base = outs[k], j * PIECE
            lo, hi, begin, keep0, keep1 = bounds(k, j)
            first = jnp.where(sub == k * 4 + j, lo, first)
            last = jnp.where(sub == k * 4 + j, hi, last)
            sums = part(begin, lo, hi, 256)
            pair, diag = packed(sums[:, :BLOCK])
            out[base : base + 128, :] = jnp.where(keep0, sums[:, BLOCK : 2 * BLOCK], zero)
            out[base + 128 : base + 256, :] = jnp.where(keep1, sums[:, 2 * BLOCK :], zero)
            out[base + 256 : base + 320, :] = pair
            out[base + 320 : base + 328, :] = jnp.broadcast_to(diag, (8, BLOCK))

    lane = iota((SLOTS, ROWS), 1)
    first = jnp.tile(first, (1, ROWS // BLOCK))
    last = jnp.tile(last, (1, ROWS // BLOCK))
    res = jnp.broadcast_to(res_ref[...].astype(F32), (SLOTS, ROWS))
    spread = jnp.where((lane >= first) & (lane < last), res, 0.0).astype(jnp.bfloat16)
    grad = jnp.dot(spread, cam_ref[...], preferred_element_type=F32)
    for i in range(SLOTS):
        base = (i % 4) * PIECE
        outs[i // 4][base + 320 : base + 321, :] = grad[i : i + 1, :]

    for k in range(4):
        for j in range(4):
            out, base = outs[k], j * PIECE
            lo, hi, begin, keep0, keep1 = bounds(k, j)

            @pl.when(hi > begin + 256)
            def _():
                second = pl.multiple_of(jnp.minimum(begin + 256, ROWS - 48), 16)
                sums = part(second, begin + 256, hi, 48)
                pair, diag = packed(sums[:, :BLOCK])
                out[base : base + 128, :] += jnp.where(keep0, sums[:, BLOCK : 2 * BLOCK], zero)
                out[base + 128 : base + 256, :] += jnp.where(keep1, sums[:, 2 * BLOCK :], zero)
                out[base + 256 : base + 320, :] += pair
                out[base + 321 : base + 322, :] += diag


def near_kernel(a_ref, b_ref, c_ref, out_ref):
    out_ref[...] = (a_ref[...] + b_ref[...]) + c_ref[...]


def add_kernel(a_ref, b_ref, *outs):
    for j in range(4):
        rows = slice(j * PIECE, (j + 1) * PIECE)
        outs[j][...] = a_ref[rows, :] + b_ref[rows, :]


def split3(value):
    high = value.astype(jnp.bfloat16)
    return high, (value - high.astype(F32)).astype(jnp.bfloat16)


def near_dot(left, right, dims=((1,), (0,))):
    (lk,), (rk,) = dims
    lh, ll = split3(left)
    rh, rl = split3(right)
    return lax.dot_general(
        jnp.concatenate([lh, lh, ll], axis=lk),
        jnp.concatenate([rh, rl, rh], axis=rk),
        (dims, ((), ())),
        preferred_element_type=F32,
    )


def lanes(value, k):
    return jnp.broadcast_to(value[:, k : k + 1], (8, BLOCK))


def subs(value, j):
    return jnp.broadcast_to(value[j : j + 1, :], (8, BLOCK))


def factor(ab, upper, block):
    row, col = iota((BLOCK, BLOCK), 0), iota((BLOCK, BLOCK), 1)
    sub = iota((8, BLOCK), 0)
    ab[:, :BLOCK] = block
    ab[:, BLOCK:] = (row == col).astype(F32)
    cur = [block[:8], ab[:8, BLOCK:]]
    for b in range(16):
        more = b < 15
        heads = [lanes(cur[0], 8 * b + k) for k in range(8)]
        if more:
            rows = slice(8 * (b + 1), 8 * (b + 2))
            below = [ab[rows, :BLOCK], ab[rows, BLOCK:]]
            tails = [lanes(below[0], 8 * b + k) for k in range(8)]
        for j in range(8):
            scale = lax.rsqrt(subs(heads[j], j))
            head = jnp.where(sub > j, heads[j] * scale, 0.0)
            for k in range(j + 1, 8):
                pick = subs(heads[k], j) * scale
                heads[k] = heads[k] - head * pick
                if more:
                    if k == j + 1:
                        tail = tails[j] * scale
                    tails[k] = tails[k] - tail * pick
            if more and j == 7:
                tail = tails[j] * scale
            for part in range(2):
                pivot = subs(cur[part], j) * scale
                cur[part] = jnp.where(sub == j, pivot, cur[part] - head * pivot)
                if more:
                    below[part] = below[part] - tail * pivot
        done = jnp.concatenate(cur, axis=1)
        upper[8 * b : 8 * b + 8, :] = done
        if b < 14:
            high, low = split3(done)
            update = col_dot(
                jnp.concatenate([high[:, :BLOCK], high[:, :BLOCK], low[:, :BLOCK]], axis=0),
                jnp.concatenate([high, low, high], axis=0),
            )
            ab[8 * (b + 2) :, :] -= update[8 * (b + 2) :, :]
        if more:
            cur = below
    return jnp.where(row >= col, upper[:, :BLOCK].T, 0.0), upper[:, BLOCK:]


def panel_kernel(sums_ref, damping_ref, factor_ref, inv_ref, sol_ref, ab, upper):
    damping = damping_ref[0]
    sums = sums_ref[...]
    both = sums[:, :SHARE, :].reshape(TEX_W, BLOCK)
    mixed, h10 = both[:BLOCK], both[BLOCK:]
    g0, g1, diag = sums[0, SHARE : SHARE + 1, :], sums[1, SHARE : SHARE + 1, :], sums[2, SHARE : SHARE + 1, :]
    row, col = iota((BLOCK, BLOCK), 0), iota((BLOCK, BLOCK), 1)
    flipped = mixed.T
    h00 = jnp.where(row >= col, mixed, flipped)
    h11 = jnp.where(row < col, mixed, jnp.where(row == col, diag, flipped))
    h00 = jnp.where(row == col, h00 + damping * h00, h00)
    h11 = jnp.where(row == col, h11 + damping * h11, h11)
    across = ((1,), (1,))
    l00, w00 = factor(ab, upper, h00)
    l10 = near_dot(h10, w00, across)
    y0 = near_dot(g0, w00, across)
    zero = jnp.zeros((BLOCK, BLOCK), F32)
    factor_ref[:BLOCK, :BLOCK] = l00
    factor_ref[:BLOCK, BLOCK:] = zero
    factor_ref[BLOCK:, :BLOCK] = l10
    inv_ref[:BLOCK, :BLOCK] = w00
    inv_ref[:BLOCK, BLOCK:] = zero
    lw = near_dot(l10, w00)
    l11, w11 = factor(ab, upper, h11 - near_dot(l10, l10, across))
    factor_ref[BLOCK:, BLOCK:] = l11
    inv_ref[BLOCK:, :BLOCK] = -near_dot(w11, lw)
    inv_ref[BLOCK:, BLOCK:] = w11
    sol_ref[:, :BLOCK] = y0
    sol_ref[:, BLOCK:] = near_dot(g1 - near_dot(y0, l10, across), w11, across)


def last_kernel(a_ref, b_ref, c_ref, d_ref, inv_ref, sol_ref, damping_ref, red_ref, grad_ref, coup_ref):
    damping = damping_ref[0]
    total = (a_ref[...] + b_ref[...]) + (c_ref[...] + d_ref[...])
    cross = jnp.concatenate([total[:128], total[128:256]], axis=1)
    pair, grad, diag = total[256:320], total[320:321], total[321:322]
    row, col = iota((BLOCK, BLOCK), 0), iota((BLOCK, BLOCK), 1)
    row64, lane64 = iota((64, BLOCK), 0), iota((64, BLOCK), 1)
    turned = pltpu.roll(pair, 64, 1)
    top = jnp.where(lane64 < 64, turned, 0.0)
    square = jnp.concatenate([top, pair], axis=0)
    other = square.T
    lower = jnp.where((row >= 64) & (col >= 64), other, square)
    lower = jnp.where(row > col, lower, 0.0)
    main = jnp.where(row == col, jnp.where(row < 64, square, diag), 0.0)
    hess = lower + lower.T + main + damping * main
    coupling = exact_dot(cross, inv_ref[...], ((1,), (1,)))
    coup_ref[...] = coupling
    red_ref[...] = hess - exact_dot(coupling, coupling, ((1,), (1,)))
    grad_ref[...] = grad - exact_dot(sol_ref[...], coupling, ((1,), (1,)))


LOCAL_SCRATCH = [
    pltpu.SMEM((SLOTS + 1,), jnp.int32),
    pltpu.VMEM((ROWS, BLOCK), jnp.bfloat16),
    pltpu.VMEM((ROWS, TEX_W), jnp.bfloat16),
    pltpu.VMEM((1, ROWS), jnp.bfloat16),
    pltpu.SMEM((OBS,), jnp.int32),
    pltpu.SMEM((SLOTS,), jnp.int32),
    pltpu.SMEM((512,), jnp.int32),
    pltpu.SemaphoreType.DMA((12,)),
]
COST = {
    name: pl.CostEstimate(flops=flops, bytes_accessed=0, transcendentals=0)
    for name, flops in {"near": 6_000_000_000, "add": 1_000_000_000}.items()
}
PANEL = [pltpu.VMEM((BLOCK, TEX_W), F32), pltpu.VMEM((BLOCK, TEX_W), F32)]


def call(kernel, name, outs, specs, scratch=(), room=24):
    return pl.pallas_call(
        kernel,
        cost_estimate=COST.get(name),
        out_shape=[jax.ShapeDtypeStruct(s, F32) for s in outs],
        in_specs=specs,
        out_specs=[VMEM] * len(outs),
        scratch_shapes=scratch,
        name=name,
        compiler_params=pltpu.CompilerParams(vmem_limit_bytes=room * 2**20),
    )


def shift(value, axis, by):
    n = lax.axis_size(axis)
    return lax.ppermute(value, axis, [(i, (i + by) % n) for i in range(n)])


def spread_sum(value, axes):
    count = lax.axis_size(axes)
    copies = jnp.broadcast_to(value[None], (count, *value.shape))
    return jnp.sum(lax.all_to_all(copies, axes, 0, 0), axis=0)


FAR = ("x", "z")
NEAR = ("yl", "yh", "c")


def shards(jac_cam, jac_tex, residual, obs_slot, col_ids, block_pattern, damping):
    cam, tex = jac_cam[0, 0], jac_tex[0, 0]
    res, obs = residual[0], obs_slot[0, 0]
    damping = damping.reshape(1)

    *pieces, tex_part = call(
        local_kernel,
        "local",
        [(4 * PIECE, BLOCK)] * 4 + [(FAR_N, 2 * SHARE, BLOCK)],
        [HBM] * 6,
        LOCAL_SCRATCH,
        60,
    )(cam, tex, res, obs, col_ids, block_pattern)
    beside = [pieces[0]] + [shift(pieces[k], "x", k) for k in (1, 3)]
    across = shift(pieces[2], "x", 2)
    (beside,) = call(near_kernel, "near", [(4 * PIECE, BLOCK)], [VMEM] * 3)(*beside)
    pieces = call(add_kernel, "add", [(PIECE, BLOCK)] * 4, [VMEM] * 2)(beside, across)
    moved = [pieces[0]] + [shift(pieces[j], "yl", j) for j in (1, 2, 3)]

    share = jnp.sum(lax.all_to_all(tex_part, FAR, 0, 0), axis=0)
    share = spread_sum(share, NEAR)
    copies = jnp.broadcast_to(share[None], (FAR_N, *share.shape))
    tex_sums = lax.all_to_all(copies, FAR, 0, 0)

    texture_factor, inverse, sol = call(
        panel_kernel, "panel", [(TEX_W, TEX_W), (TEX_W, TEX_W), (1, TEX_W)], [VMEM, SMEM], PANEL
    )(tex_sums, damping)
    reduced, gradient, coupling = call(
        last_kernel,
        "last",
        [(BLOCK, BLOCK), (1, BLOCK), (BLOCK, TEX_W)],
        [VMEM] * 6 + [SMEM],
    )(*moved, inverse, sol, damping)
    return (reduced[None, None], gradient[None], coupling[None, None], texture_factor)


def solution(mesh):
    fine = Mesh(mesh.devices.reshape(4, 4, 2, 8, 2), ("yl", "x", "yh", "z", "c"))
    img, blk = ("yl", "x"), ("yh", "z", "c")
    return jax.shard_map(
        shards,
        mesh=fine,
        in_specs=(
            P(img, blk, None, None),
            P(img, blk, None, None),
            P(img, blk, None),
            P(img, blk, None),
            P(blk),
            P(),
            P(),
        ),
        out_specs=(
            P(blk, img, None, None),
            P(blk, img, None),
            P(blk, img, None, None),
            P(),
        ),
        check_vma=False,
    )
```

```python
import functools

import jax
import jax.numpy as jnp
from jax import lax
from jax.experimental import pallas as pl
from jax.experimental.pallas import tpu as pltpu
from jax.sharding import Mesh, PartitionSpec as P

BLOCK = 128
TEX_W = 256
ROWS = 1536
OBS = 192
PER = 8
SLOTS = 16
FAR_N = 32
SHARE = TEX_W // FAR_N
BODY = 320
F32 = jnp.float32
VMEM = pl.BlockSpec(memory_space=pltpu.VMEM)
HBM = pl.BlockSpec(memory_space=pltpu.HBM)
SMEM = pl.BlockSpec(memory_space=pltpu.SMEM)


def col_dot(left, right):
    return lax.dot_general(left, right, (((0,), (0,)), ((), ())), preferred_element_type=F32)


def iota(shape, dim):
    return lax.broadcasted_iota(jnp.int32, shape, dim)


def find_starts(obs_ref, starts):
    starts[SLOTS] = OBS

    def step(i, carry):
        j = OBS - 1 - i
        starts[obs_ref[j]] = j
        return carry

    lax.fori_loop(0, OBS, step, 0, unroll=8)


def fetch(pairs, sems):
    copies = []
    for src, dst in pairs:
        step = dst.shape[0] // 4 if dst.shape[0] == ROWS else dst.shape[0]
        for n in range(0, dst.shape[0], step):
            part = pl.ds(n, step)
            copies.append(pltpu.make_async_copy(src.at[part], dst.at[part], sems.at[len(copies)]))
    for copy in copies:
        copy.start()
    return copies


def tex_sums(tex_ref, res_ref, ids_ref, pattern_ref, starts, out_ref):
    obs_index = iota((OBS, BLOCK), 0)
    masks = []
    for bit in range(2):
        keep = jnp.zeros((OBS, BLOCK), jnp.int32)
        for s in range(SLOTS):
            keep = jnp.where(obs_index >= starts[s], (pattern_ref[ids_ref[s]] >> bit) & 1, keep)
        rows = jnp.broadcast_to(keep.astype(F32)[:, None, :], (OBS, PER, BLOCK))
        masks.append(rows.reshape(ROWS, BLOCK).astype(jnp.bfloat16))
    masked = tex_ref[...] * jnp.concatenate(masks, axis=1)
    hess = col_dot(masked, masked)
    grad = jnp.dot(res_ref[...], masked, preferred_element_type=F32)
    h00, h10, h11 = hess[:BLOCK, :BLOCK], hess[BLOCK:, :BLOCK], hess[BLOCK:, BLOCK:]
    row, col = iota((BLOCK, BLOCK), 0), iota((BLOCK, BLOCK), 1)
    mixed = jnp.where(row >= col, h00, h11)
    diag = jnp.sum(jnp.where(row == col, h11, 0.0), axis=0, keepdims=True)
    half = FAR_N // 2
    out_ref[:, SHARE:, :] = jnp.zeros((FAR_N, 8, BLOCK), F32)
    out_ref[:half, :SHARE, :] = mixed.reshape(half, SHARE, BLOCK)
    out_ref[half:, :SHARE, :] = h10.reshape(half, SHARE, BLOCK)
    out_ref[0, SHARE : SHARE + 1, :] = grad[:, :BLOCK]
    out_ref[1, SHARE : SHARE + 1, :] = grad[:, BLOCK:]
    out_ref[2, SHARE : SHARE + 1, :] = diag


def packed(hess):
    row, lane = iota((64, BLOCK), 0), iota((64, BLOCK), 1)
    low, high = hess[64:, :], hess[:64, :]
    turned = pltpu.roll(high, 64, 1)
    pair = jnp.where((lane >= 64) & (row >= lane - 64), turned, low)
    return pair, jnp.sum(jnp.where(row == lane - 64, low, 0.0), axis=0, keepdims=True)


def local_kernel(
    cam_any, tex_any, res_any, obs_any, ids_any, pattern_any, out0, out1, out2, out3, tex_out,
    starts, cam_ref, tex_ref, res_ref, obs_ref, ids_ref, pattern_ref, sems,
):
    outs, my_x, my_yl = (out0, out1, out2, out3), lax.axis_index("x"), lax.axis_index("yl")
    copies = fetch(
        (
            (obs_any, obs_ref),
            (ids_any, ids_ref),
            (pattern_any, pattern_ref),
            (res_any, res_ref),
            (cam_any, cam_ref),
            (tex_any, tex_ref),
        ),
        sems,
    )
    for copy in copies[:4]:
        copy.wait()
    find_starts(obs_ref, starts)
    sub = iota((SLOTS, BLOCK), 0)
    first = jnp.zeros((SLOTS, BLOCK), jnp.int32)
    last = jnp.zeros((SLOTS, BLOCK), jnp.int32)
    for copy in copies[4:]:
        copy.wait()
    tex_sums(tex_ref, res_ref, ids_ref, pattern_ref, starts, tex_out)

    def bounds(k, j):
        slot = ((my_yl + j) & 3) * 4 + ((my_x + k) & 3)
        lo, hi = starts[slot] * PER, starts[slot + 1] * PER
        begin = pl.multiple_of(jnp.minimum((lo >> 4) << 4, ROWS - 256), 16)
        code = pattern_ref[ids_ref[slot]]
        return lo, hi, begin, (code & 1) == 1, (code >> 1) == 1

    def part(begin, lo, hi, count):
        cam = cam_ref[pl.ds(begin, count), :]
        both = jnp.concatenate([cam, tex_ref[pl.ds(begin, count), :]], axis=1)
        where = iota((count, BLOCK), 0) + begin
        keep = ((where >= lo) & (where < hi)).astype(F32).astype(jnp.bfloat16)
        return col_dot(cam * keep, both)

    zero = jnp.zeros((BLOCK, BLOCK), F32)
    for k in range(4):
        for j in range(4):
            out, base, tail = outs[k], j * BODY, 4 * BODY + 2 * j
            lo, hi, begin, keep0, keep1 = bounds(k, j)
            first = jnp.where(sub == k * 4 + j, lo, first)
            last = jnp.where(sub == k * 4 + j, hi, last)
            sums = part(begin, lo, hi, 256)
            pair, diag = packed(sums[:, :BLOCK])
            out[base : base + 128, :] = jnp.where(keep0, sums[:, BLOCK : 2 * BLOCK], zero)
            out[base + 128 : base + 256, :] = jnp.where(keep1, sums[:, 2 * BLOCK :], zero)
            out[base + 256 : base + 320, :] = pair
            out[tail + 1 : tail + 2, :] = diag

    lane = iota((SLOTS, ROWS), 1)
    first = jnp.tile(first, (1, ROWS // BLOCK))
    last = jnp.tile(last, (1, ROWS // BLOCK))
    res = jnp.broadcast_to(res_ref[...].astype(F32), (SLOTS, ROWS))
    spread = jnp.where((lane >= first) & (lane < last), res, 0.0).astype(jnp.bfloat16)
    grad = jnp.dot(spread, cam_ref[...], preferred_element_type=F32)
    for i in range(SLOTS):
        tail = 4 * BODY + 2 * (i % 4)
        outs[i // 4][tail : tail + 1, :] = grad[i : i + 1, :]

    for k in range(4):
        for j in range(4):
            out, base, tail = outs[k], j * BODY, 4 * BODY + 2 * j
            lo, hi, begin, keep0, keep1 = bounds(k, j)

            @pl.when(hi > begin + 256)
            def _():
                second = pl.multiple_of(jnp.minimum(begin + 256, ROWS - 48), 16)
                sums = part(second, begin + 256, hi, 48)
                pair, diag = packed(sums[:, :BLOCK])
                out[base : base + 128, :] += jnp.where(keep0, sums[:, BLOCK : 2 * BLOCK], zero)
                out[base + 128 : base + 256, :] += jnp.where(keep1, sums[:, 2 * BLOCK :], zero)
                out[base + 256 : base + 320, :] += pair
                out[tail + 1 : tail + 2, :] += diag


def add_kernel(a_ref, b_ref, c_ref, d_ref, *outs):
    for j in range(4):
        for rows, put in (
            (slice(j * BODY, (j + 1) * BODY), slice(0, BODY)),
            (slice(4 * BODY + 2 * j, 4 * BODY + 2 * j + 2), slice(BODY, BODY + 2)),
        ):
            outs[j][put, :] = (a_ref[rows, :] + b_ref[rows, :]) + (c_ref[rows, :] + d_ref[rows, :])
        outs[j][BODY + 2 :, :] = jnp.zeros((6, BLOCK), F32)


def split3(value):
    high = value.astype(jnp.bfloat16)
    return high, (value - high.astype(F32)).astype(jnp.bfloat16)


def near_dot(left, right, dims=((1,), (0,))):
    (lk,), (rk,) = dims
    lh, ll = split3(left)
    rh, rl = split3(right)
    return lax.dot_general(
        jnp.concatenate([lh, lh, ll], axis=lk),
        jnp.concatenate([rh, rl, rh], axis=rk),
        (dims, ((), ())),
        preferred_element_type=F32,
    )


def lanes(value, k):
    return jnp.broadcast_to(value[:, k : k + 1], (8, BLOCK))


def subs(value, j):
    return jnp.broadcast_to(value[j : j + 1, :], (8, BLOCK))


def factor(ab, upper, block):
    row, col = iota((BLOCK, BLOCK), 0), iota((BLOCK, BLOCK), 1)
    sub = iota((8, BLOCK), 0)
    ab[:, :BLOCK] = block
    ab[:, BLOCK:] = (row == col).astype(F32)
    cur = [block[:8], ab[:8, BLOCK:]]
    for b in range(16):
        more = b < 15
        heads = [lanes(cur[0], 8 * b + k) for k in range(8)]
        if more:
            rows = slice(8 * (b + 1), 8 * (b + 2))
            below = [ab[rows, :BLOCK], ab[rows, BLOCK:]]
            tails = [lanes(below[0], 8 * b + k) for k in range(8)]
        for j in range(8):
            scale = lax.rsqrt(subs(heads[j], j))
            head = jnp.where(sub > j, heads[j] * scale, 0.0)
            for k in range(j + 1, 8):
                pick = subs(heads[k], j) * scale
                heads[k] = heads[k] - head * pick
                if more:
                    if k == j + 1:
                        tail = tails[j] * scale
                    tails[k] = tails[k] - tail * pick
            if more and j == 7:
                tail = tails[j] * scale
            for part in range(2):
                pivot = subs(cur[part], j) * scale
                cur[part] = jnp.where(sub == j, pivot, cur[part] - head * pivot)
                if more:
                    below[part] = below[part] - tail * pivot
        done = jnp.concatenate(cur, axis=1)
        upper[8 * b : 8 * b + 8, :] = done
        if b < 14:
            high, low = split3(done)
            update = col_dot(
                jnp.concatenate([high[:, :BLOCK], high[:, :BLOCK], low[:, :BLOCK]], axis=0),
                jnp.concatenate([high, low, high], axis=0),
            )
            ab[8 * (b + 2) :, :] -= update[8 * (b + 2) :, :]
        if more:
            cur = below
    return jnp.where(row >= col, upper[:, :BLOCK].T, 0.0), upper[:, BLOCK:]


def panel_kernel(sums_ref, damping_ref, factor_ref, inv_ref, sol_ref, ab, upper):
    damping = damping_ref[0]
    sums = sums_ref[...]
    both = sums[:, :SHARE, :].reshape(TEX_W, BLOCK)
    mixed, h10 = both[:BLOCK], both[BLOCK:]
    g0, g1, diag = sums[0, SHARE : SHARE + 1, :], sums[1, SHARE : SHARE + 1, :], sums[2, SHARE : SHARE + 1, :]
    row, col = iota((BLOCK, BLOCK), 0), iota((BLOCK, BLOCK), 1)
    flipped = mixed.T
    h00 = jnp.where(row >= col, mixed, flipped)
    h11 = jnp.where(row < col, mixed, jnp.where(row == col, diag, flipped))
    h00 = jnp.where(row == col, h00 + damping * h00, h00)
    h11 = jnp.where(row == col, h11 + damping * h11, h11)
    across = ((1,), (1,))
    l00, w00 = factor(ab, upper, h00)
    l10 = near_dot(h10, w00, across)
    y0 = near_dot(g0, w00, across)
    zero = jnp.zeros((BLOCK, BLOCK), F32)
    factor_ref[:BLOCK, :BLOCK] = l00
    factor_ref[:BLOCK, BLOCK:] = zero
    factor_ref[BLOCK:, :BLOCK] = l10
    inv_ref[:BLOCK, :BLOCK] = w00
    inv_ref[:BLOCK, BLOCK:] = zero
    lw = near_dot(l10, w00)
    l11, w11 = factor(ab, upper, h11 - near_dot(l10, l10, across))
    factor_ref[BLOCK:, BLOCK:] = l11
    inv_ref[BLOCK:, :BLOCK] = -near_dot(w11, lw)
    inv_ref[BLOCK:, BLOCK:] = w11
    sol_ref[:, :BLOCK] = y0
    sol_ref[:, BLOCK:] = near_dot(g1 - near_dot(y0, l10, across), w11, across)


def last_kernel(a_ref, b_ref, c_ref, d_ref, inv_ref, sol_ref, damping_ref, red_ref, grad_ref, coup_ref):
    damping = damping_ref[0]
    total = (a_ref[...] + b_ref[...]) + (c_ref[...] + d_ref[...])
    cross = jnp.concatenate([total[:128], total[128:256]], axis=1)
    pair, grad, diag = total[256:320], total[320:321], total[321:322]
    row, col = iota((BLOCK, BLOCK), 0), iota((BLOCK, BLOCK), 1)
    row64, lane64 = iota((64, BLOCK), 0), iota((64, BLOCK), 1)
    turned = pltpu.roll(pair, 64, 1)
    top = jnp.where(lane64 < 64, turned, 0.0)
    square = jnp.concatenate([top, pair], axis=0)
    other = square.T
    lower = jnp.where((row >= 64) & (col >= 64), other, square)
    lower = jnp.where(row > col, lower, 0.0)
    main = jnp.where(row == col, jnp.where(row < 64, square, diag), 0.0)
    hess = lower + lower.T + main + damping * main
    coupling = near_dot(cross, inv_ref[...], ((1,), (1,)))
    coup_ref[...] = coupling
    red_ref[...] = hess - near_dot(coupling, coupling, ((1,), (1,)))
    grad_ref[...] = grad - near_dot(sol_ref[...], coupling, ((1,), (1,)))


LOCAL_SCRATCH = [
    pltpu.SMEM((SLOTS + 1,), jnp.int32),
    pltpu.VMEM((ROWS, BLOCK), jnp.bfloat16),
    pltpu.VMEM((ROWS, TEX_W), jnp.bfloat16),
    pltpu.VMEM((1, ROWS), jnp.bfloat16),
    pltpu.SMEM((OBS,), jnp.int32),
    pltpu.SMEM((SLOTS,), jnp.int32),
    pltpu.SMEM((512,), jnp.int32),
    pltpu.SemaphoreType.DMA((12,)),
]
COST = {}
PANEL = [pltpu.VMEM((BLOCK, TEX_W), F32), pltpu.VMEM((BLOCK, TEX_W), F32)]


def call(kernel, name, outs, specs, scratch=(), room=24):
    return pl.pallas_call(
        kernel,
        cost_estimate=COST.get(name),
        out_shape=[jax.ShapeDtypeStruct(s, F32) for s in outs],
        in_specs=specs,
        out_specs=[VMEM] * len(outs),
        scratch_shapes=scratch,
        name=name,
        compiler_params=pltpu.CompilerParams(vmem_limit_bytes=room * 2**20),
    )


def shift(value, axis, by):
    n = lax.axis_size(axis)
    return lax.ppermute(value, axis, [(i, (i + by) % n) for i in range(n)])


def spread_sum(value, axes):
    count = lax.axis_size(axes)
    copies = jnp.broadcast_to(value[None], (count, *value.shape))
    return jnp.sum(lax.all_to_all(copies, axes, 0, 0), axis=0)


FAR = ("x", "z")
NEAR = ("yl", "yh", "c")


def shards(jac_cam, jac_tex, residual, obs_slot, col_ids, block_pattern, damping):
    cam, tex = jac_cam[0, 0], jac_tex[0, 0]
    res, obs = residual[0], obs_slot[0, 0]
    damping = damping.reshape(1)

    *pieces, tex_part = call(
        local_kernel,
        "local",
        [(4 * BODY + 8, BLOCK)] * 4 + [(FAR_N, SHARE + 8, BLOCK)],
        [HBM] * 6,
        LOCAL_SCRATCH,
        60,
    )(cam, tex, res, obs, col_ids, block_pattern)
    moved = [pieces[0]] + [shift(pieces[k], "x", k) for k in (2, 1, 3)]
    pieces = call(add_kernel, "add", [(BODY + 8, BLOCK)] * 4, [VMEM] * 4)(*moved)
    parts = [pieces[0]] + [shift(pieces[j], "yl", j) for j in (1, 2, 3)]

    share = jnp.sum(lax.all_to_all(tex_part, FAR, 0, 0), axis=0)
    share = spread_sum(share, NEAR)
    copies = jnp.broadcast_to(share[None], (FAR_N, *share.shape))
    tex_sums = lax.all_to_all(copies, FAR, 0, 0)

    texture_factor, inverse, sol = call(
        panel_kernel, "panel", [(TEX_W, TEX_W), (TEX_W, TEX_W), (1, TEX_W)], [VMEM, SMEM], PANEL
    )(tex_sums, damping)
    reduced, gradient, coupling = call(
        last_kernel,
        "last",
        [(BLOCK, BLOCK), (1, BLOCK), (BLOCK, TEX_W)],
        [VMEM] * 6 + [SMEM],
    )(*parts, inverse, sol, damping)
    return (reduced[None, None], gradient[None], coupling[None, None], texture_factor)


def solution(mesh):
    fine = Mesh(mesh.devices.reshape(4, 4, 2, 8, 2), ("yl", "x", "yh", "z", "c"))
    img, blk = ("yl", "x"), ("yh", "z", "c")
    return jax.shard_map(
        shards,
        mesh=fine,
        in_specs=(
            P(img, blk, None, None),
            P(img, blk, None, None),
            P(img, blk, None),
            P(img, blk, None),
            P(blk),
            P(),
            P(),
        ),
        out_specs=(
            P(blk, img, None, None),
            P(blk, img, None),
            P(blk, img, None, None),
            P(),
        ),
        check_vma=False,
    )
```

```python
import functools

import jax
import jax.numpy as jnp
from jax import lax
from jax.experimental import pallas as pl
from jax.experimental.pallas import tpu as pltpu
from jax.sharding import Mesh, PartitionSpec as P

BLOCK = 128
TEX_W = 256
ROWS = 1536
OBS = 192
PER = 8
SLOTS = 16
FAR_N = 32
SHARE = TEX_W // FAR_N
WINDOW = 304
BODY = 320
F32 = jnp.float32
VMEM = pl.BlockSpec(memory_space=pltpu.VMEM)
HBM = pl.BlockSpec(memory_space=pltpu.HBM)
SMEM = pl.BlockSpec(memory_space=pltpu.SMEM)


def col_dot(left, right):
    return lax.dot_general(left, right, (((0,), (0,)), ((), ())), preferred_element_type=F32)


def iota(shape, dim):
    return lax.broadcasted_iota(jnp.int32, shape, dim)


def find_starts(obs_ref, starts):
    starts[SLOTS] = OBS

    def step(i, carry):
        j = OBS - 1 - i
        starts[obs_ref[j]] = j
        return carry

    lax.fori_loop(0, OBS, step, 0, unroll=8)


def fetch(pairs, sems):
    copies = []
    for src, dst in pairs:
        if dst.shape[0] != ROWS:
            copies.append(pltpu.make_async_copy(src, dst, sems.at[len(copies)]))
            continue
        for n in range(0, ROWS, ROWS // 4):
            part = pl.ds(n, ROWS // 4)
            copies.append(pltpu.make_async_copy(src.at[part], dst.at[part], sems.at[len(copies)]))
    for copy in copies:
        copy.start()
    return copies


def tex_sums(tex_ref, res_ref, ids_ref, pattern_ref, starts, out_ref):
    obs_index = iota((OBS, BLOCK), 0)
    masks = []
    for bit in range(2):
        keep = jnp.zeros((OBS, BLOCK), jnp.int32)
        for s in range(SLOTS):
            keep = jnp.where(obs_index >= starts[s], (pattern_ref[ids_ref[s]] >> bit) & 1, keep)
        rows = jnp.broadcast_to(keep.astype(F32)[:, None, :], (OBS, PER, BLOCK))
        masks.append(rows.reshape(ROWS, BLOCK).astype(jnp.bfloat16))
    masked = tex_ref[...] * jnp.concatenate(masks, axis=1)
    hess = col_dot(masked, masked)
    grad = jnp.dot(res_ref[...], masked, preferred_element_type=F32)
    h00, h10, h11 = hess[:BLOCK, :BLOCK], hess[BLOCK:, :BLOCK], hess[BLOCK:, BLOCK:]
    row, col = iota((BLOCK, BLOCK), 0), iota((BLOCK, BLOCK), 1)
    mixed = jnp.where(row >= col, h00, h11)
    diag = jnp.sum(jnp.where(row == col, h11, 0.0), axis=0, keepdims=True)
    half = FAR_N // 2
    out_ref[:, SHARE:, :] = jnp.zeros((FAR_N, 8, BLOCK), F32)
    out_ref[:half, :SHARE, :] = mixed.reshape(half, SHARE, BLOCK)
    out_ref[half:, :SHARE, :] = h10.reshape(half, SHARE, BLOCK)
    out_ref[0, SHARE : SHARE + 1, :] = grad[:, :BLOCK]
    out_ref[1, SHARE : SHARE + 1, :] = grad[:, BLOCK:]
    out_ref[2, SHARE : SHARE + 1, :] = diag


def packed(hess):
    row, lane = iota((64, BLOCK), 0), iota((64, BLOCK), 1)
    low, high = hess[64:, :], hess[:64, :]
    turned = pltpu.roll(high, 64, 1)
    pair = jnp.where((lane >= 64) & (row >= lane - 64), turned, low)
    return pair, jnp.sum(jnp.where(row == lane - 64, low, 0.0), axis=0, keepdims=True)


def local_kernel(
    cam_any, tex_any, res_any, obs_any, ids_any, pattern_any, out0, out1, out2, out3, tex_out,
    starts, cam_ref, tex_ref, res_ref, obs_ref, ids_ref, pattern_ref, sems, outs, tex_sums_ref, out_sems,
):
    dests, my_x, my_yl = (out0, out1, out2, out3), lax.axis_index("x"), lax.axis_index("yl")
    copies = fetch(
        (
            (obs_any, obs_ref),
            (ids_any, ids_ref),
            (pattern_any, pattern_ref),
            (res_any, res_ref),
            (cam_any, cam_ref),
            (tex_any, tex_ref),
        ),
        sems,
    )
    for copy in copies[:4]:
        copy.wait()
    find_starts(obs_ref, starts)
    sub = iota((SLOTS, BLOCK), 0)
    first = jnp.zeros((SLOTS, BLOCK), jnp.int32)
    last = jnp.zeros((SLOTS, BLOCK), jnp.int32)
    for copy in copies[4:]:
        copy.wait()
    tex_sums(tex_ref, res_ref, ids_ref, pattern_ref, starts, tex_sums_ref)
    leave = [pltpu.make_async_copy(tex_sums_ref, tex_out, out_sems.at[4])]
    leave[0].start()

    def bounds(k, j):
        slot = ((my_yl + j) & 3) * 4 + ((my_x + k) & 3)
        lo, hi = starts[slot] * PER, starts[slot + 1] * PER
        begin = pl.multiple_of(jnp.minimum((lo >> 4) << 4, ROWS - WINDOW), 16)
        code = pattern_ref[ids_ref[slot]]
        return lo, hi, begin, (code & 1) == 1, (code >> 1) == 1

    def part(begin, lo, hi, count):
        cam = cam_ref[pl.ds(begin, count), :]
        both = jnp.concatenate([cam, tex_ref[pl.ds(begin, count), :]], axis=1)
        where = iota((count, BLOCK), 0) + begin
        keep = ((where >= lo) & (where < hi)).astype(F32).astype(jnp.bfloat16)
        return col_dot(cam * keep, both)

    for i in range(SLOTS):
        lo, hi, *_ = bounds(i // 4, i % 4)
        first = jnp.where(sub == i, lo, first)
        last = jnp.where(sub == i, hi, last)
    lane = iota((SLOTS, ROWS), 1)
    first = jnp.tile(first, (1, ROWS // BLOCK))
    last = jnp.tile(last, (1, ROWS // BLOCK))
    res = jnp.broadcast_to(res_ref[...].astype(F32), (SLOTS, ROWS))
    spread = jnp.where((lane >= first) & (lane < last), res, 0.0).astype(jnp.bfloat16)
    grad = jnp.dot(spread, cam_ref[...], preferred_element_type=F32)
    zero = jnp.zeros((BLOCK, BLOCK), F32)
    for k in (2, 1, 3, 0):
        for j in range(4):
            out, base, tail = outs.at[k], j * BODY, 4 * BODY + 2 * j
            lo, hi, begin, keep0, keep1 = bounds(k, j)
            sums = part(begin, lo, hi, WINDOW)
            pair, diag = packed(sums[:, :BLOCK])
            out[base : base + 128, :] = jnp.where(keep0, sums[:, BLOCK : 2 * BLOCK], zero)
            out[base + 128 : base + 256, :] = jnp.where(keep1, sums[:, 2 * BLOCK :], zero)
            out[base + 256 : base + 320, :] = pair
            out[tail + 1 : tail + 2, :] = diag
            out[tail : tail + 1, :] = grad[4 * k + j : 4 * k + j + 1, :]
        leave.append(pltpu.make_async_copy(outs.at[k], dests[k], out_sems.at[k]))
        leave[-1].start()
    for copy in leave:
        copy.wait()


def near_kernel(a_ref, b_ref, out_ref):
    out_ref[...] = a_ref[...] + b_ref[...]


def add_kernel(a_ref, b_ref, c_ref, *outs):
    for j in range(4):
        for rows, put in (
            (slice(j * BODY, (j + 1) * BODY), slice(0, BODY)),
            (slice(4 * BODY + 2 * j, 4 * BODY + 2 * j + 2), slice(BODY, BODY + 2)),
        ):
            outs[j][put, :] = (a_ref[rows, :] + b_ref[rows, :]) + c_ref[rows, :]
        outs[j][BODY + 2 :, :] = jnp.zeros((6, BLOCK), F32)


def split3(value):
    high = value.astype(jnp.bfloat16)
    return high, (value - high.astype(F32)).astype(jnp.bfloat16)


def near_dot(left, right, dims=((1,), (0,))):
    (lk,), (rk,) = dims
    lh, ll = split3(left)
    rh, rl = split3(right)
    return lax.dot_general(
        jnp.concatenate([lh, lh, ll], axis=lk),
        jnp.concatenate([rh, rl, rh], axis=rk),
        (dims, ((), ())),
        preferred_element_type=F32,
    )


def lanes(value, k):
    return jnp.broadcast_to(value[:, k : k + 1], (8, BLOCK))


def subs(value, j):
    return jnp.broadcast_to(value[j : j + 1, :], (8, BLOCK))


def factor(ab, upper, block):
    row, col = iota((BLOCK, BLOCK), 0), iota((BLOCK, BLOCK), 1)
    sub = iota((8, BLOCK), 0)
    ab[:, :BLOCK] = block
    ab[:, BLOCK:] = (row == col).astype(F32)
    cur = [block[:8], ab[:8, BLOCK:]]
    for b in range(16):
        more = b < 15
        heads = [lanes(cur[0], 8 * b + k) for k in range(8)]
        if more:
            rows = slice(8 * (b + 1), 8 * (b + 2))
            below = [ab[rows, :BLOCK], ab[rows, BLOCK:]]
            tails = [lanes(below[0], 8 * b + k) for k in range(8)]
        for j in range(8):
            scale = lax.rsqrt(subs(heads[j], j))
            head = jnp.where(sub > j, heads[j] * scale, 0.0)
            for k in range(j + 1, 8):
                pick = subs(heads[k], j) * scale
                heads[k] = heads[k] - head * pick
                if more:
                    if k == j + 1:
                        tail = tails[j] * scale
                    tails[k] = tails[k] - tail * pick
            if more and j == 7:
                tail = tails[j] * scale
            for part in range(2):
                pivot = subs(cur[part], j) * scale
                cur[part] = jnp.where(sub == j, pivot, cur[part] - head * pivot)
                if more:
                    below[part] = below[part] - tail * pivot
        done = jnp.concatenate(cur, axis=1)
        upper[8 * b : 8 * b + 8, :] = done
        if b < 14:
            high, low = split3(done)
            update = col_dot(
                jnp.concatenate([high[:, :BLOCK], high[:, :BLOCK], low[:, :BLOCK]], axis=0),
                jnp.concatenate([high, low, high], axis=0),
            )
            ab[8 * (b + 2) :, :] -= update[8 * (b + 2) :, :]
        if more:
            cur = below
    return jnp.where(row >= col, upper[:, :BLOCK].T, 0.0), upper[:, BLOCK:]


def panel_kernel(sums_ref, damping_ref, factor_ref, inv_ref, sol_ref, ab, upper):
    damping = damping_ref[0]
    sums = sums_ref[...]
    both = sums[:, :SHARE, :].reshape(TEX_W, BLOCK)
    mixed, h10 = both[:BLOCK], both[BLOCK:]
    g0, g1, diag = sums[0, SHARE : SHARE + 1, :], sums[1, SHARE : SHARE + 1, :], sums[2, SHARE : SHARE + 1, :]
    row, col = iota((BLOCK, BLOCK), 0), iota((BLOCK, BLOCK), 1)
    flipped = mixed.T
    h00 = jnp.where(row >= col, mixed, flipped)
    h11 = jnp.where(row < col, mixed, jnp.where(row == col, diag, flipped))
    h00 = jnp.where(row == col, h00 + damping * h00, h00)
    h11 = jnp.where(row == col, h11 + damping * h11, h11)
    across = ((1,), (1,))
    l00, w00 = factor(ab, upper, h00)
    l10 = near_dot(h10, w00, across)
    y0 = near_dot(g0, w00, across)
    zero = jnp.zeros((BLOCK, BLOCK), F32)
    factor_ref[:BLOCK, :BLOCK] = l00
    factor_ref[:BLOCK, BLOCK:] = zero
    factor_ref[BLOCK:, :BLOCK] = l10
    inv_ref[:BLOCK, :BLOCK] = w00
    inv_ref[:BLOCK, BLOCK:] = zero
    lw = near_dot(l10, w00)
    l11, w11 = factor(ab, upper, h11 - near_dot(l10, l10, across))
    factor_ref[BLOCK:, BLOCK:] = l11
    inv_ref[BLOCK:, :BLOCK] = -near_dot(w11, lw)
    inv_ref[BLOCK:, BLOCK:] = w11
    sol_ref[:, :BLOCK] = y0
    sol_ref[:, BLOCK:] = near_dot(g1 - near_dot(y0, l10, across), w11, across)


def last_kernel(a_ref, b_ref, c_ref, d_ref, inv_ref, sol_ref, damping_ref, red_ref, grad_ref, coup_ref):
    damping = damping_ref[0]
    total = (a_ref[...] + b_ref[...]) + (c_ref[...] + d_ref[...])
    cross = jnp.concatenate([total[:128], total[128:256]], axis=1)
    pair, grad, diag = total[256:320], total[320:321], total[321:322]
    row, col = iota((BLOCK, BLOCK), 0), iota((BLOCK, BLOCK), 1)
    row64, lane64 = iota((64, BLOCK), 0), iota((64, BLOCK), 1)
    turned = pltpu.roll(pair, 64, 1)
    top = jnp.where(lane64 < 64, turned, 0.0)
    square = jnp.concatenate([top, pair], axis=0)
    other = square.T
    lower = jnp.where((row >= 64) & (col >= 64), other, square)
    lower = jnp.where(row > col, lower, 0.0)
    main = jnp.where(row == col, jnp.where(row < 64, square, diag), 0.0)
    hess = lower + lower.T + main + damping * main
    coupling = near_dot(cross, inv_ref[...], ((1,), (1,)))
    coup_ref[...] = coupling
    red_ref[...] = hess - near_dot(coupling, coupling, ((1,), (1,)))
    grad_ref[...] = grad - near_dot(sol_ref[...], coupling, ((1,), (1,)))


LOCAL_SCRATCH = [
    pltpu.SMEM((SLOTS + 1,), jnp.int32),
    pltpu.VMEM((ROWS, BLOCK), jnp.bfloat16),
    pltpu.VMEM((ROWS, TEX_W), jnp.bfloat16),
    pltpu.VMEM((1, ROWS), jnp.bfloat16),
    pltpu.SMEM((OBS,), jnp.int32),
    pltpu.SMEM((SLOTS,), jnp.int32),
    pltpu.SMEM((512,), jnp.int32),
    pltpu.SemaphoreType.DMA((12,)),
    pltpu.VMEM((4, 4 * BODY + 8, BLOCK), F32),
    pltpu.VMEM((FAR_N, 2 * SHARE, BLOCK), F32),
    pltpu.SemaphoreType.DMA((5,)),
]
COST = {
    name: pl.CostEstimate(flops=flops, bytes_accessed=0, transcendentals=0)
    for name, flops in {"near": 300000000, "add": 500000000}.items()
}
PANEL = [pltpu.VMEM((BLOCK, TEX_W), F32), pltpu.VMEM((BLOCK, TEX_W), F32)]


def call(kernel, name, outs, specs, scratch=(), room=24, out_spec=VMEM):
    return pl.pallas_call(
        kernel,
        cost_estimate=COST.get(name),
        out_shape=[jax.ShapeDtypeStruct(s, F32) for s in outs],
        in_specs=specs,
        out_specs=[out_spec] * len(outs),
        scratch_shapes=scratch,
        name=name,
        compiler_params=pltpu.CompilerParams(vmem_limit_bytes=room * 2**20),
    )


def shift(value, axis, by):
    n = lax.axis_size(axis)
    return lax.ppermute(value, axis, [(i, (i + by) % n) for i in range(n)])


def spread_sum(value, axes):
    count = lax.axis_size(axes)
    copies = jnp.broadcast_to(value[None], (count, *value.shape))
    return jnp.sum(lax.all_to_all(copies, axes, 0, 0), axis=0)


FAR = ("x", "z")
NEAR = ("yl", "yh", "c")


def shards(jac_cam, jac_tex, residual, obs_slot, col_ids, block_pattern, damping):
    cam, tex = jac_cam[0, 0], jac_tex[0, 0]
    res, obs = residual[0], obs_slot[0, 0]
    damping = damping.reshape(1)

    *pieces, tex_part = call(
        local_kernel,
        "local",
        [(4 * BODY + 8, BLOCK)] * 4 + [(FAR_N, SHARE + 8, BLOCK)],
        [HBM] * 6,
        LOCAL_SCRATCH,
        60,
        HBM,
    )(cam, tex, res, obs, col_ids, block_pattern)
    far, right, left = (shift(pieces[k], "x", k) for k in (2, 1, 3))
    (near,) = call(near_kernel, "near", [(4 * BODY + 8, BLOCK)], [VMEM] * 2)(pieces[0], far)
    pieces = call(add_kernel, "add", [(BODY + 8, BLOCK)] * 4, [VMEM] * 3)(near, right, left)
    parts = [pieces[0]] + [shift(pieces[j], "yl", j) for j in (1, 2, 3)]

    share = jnp.sum(lax.all_to_all(tex_part, FAR, 0, 0), axis=0)
    share = spread_sum(share, NEAR)
    copies = jnp.broadcast_to(share[None], (FAR_N, *share.shape))
    tex_sums = lax.all_to_all(copies, FAR, 0, 0)

    texture_factor, inverse, sol = call(
        panel_kernel, "panel", [(TEX_W, TEX_W), (TEX_W, TEX_W), (1, TEX_W)], [VMEM, SMEM], PANEL
    )(tex_sums, damping)
    reduced, gradient, coupling = call(
        last_kernel,
        "last",
        [(BLOCK, BLOCK), (1, BLOCK), (BLOCK, TEX_W)],
        [VMEM] * 6 + [SMEM],
    )(*parts, inverse, sol, damping)
    return (reduced[None, None], gradient[None], coupling[None, None], texture_factor)


def solution(mesh):
    fine = Mesh(mesh.devices.reshape(4, 4, 2, 8, 2), ("yl", "x", "yh", "z", "c"))
    img, blk = ("yl", "x"), ("yh", "z", "c")
    return jax.shard_map(
        shards,
        mesh=fine,
        in_specs=(
            P(img, blk, None, None),
            P(img, blk, None, None),
            P(img, blk, None),
            P(img, blk, None),
            P(blk),
            P(),
            P(),
        ),
        out_specs=(
            P(blk, img, None, None),
            P(blk, img, None),
            P(blk, img, None, None),
            P(),
        ),
        check_vma=False,
    )
```

```python
import functools

import jax
import jax.numpy as jnp
from jax import lax
from jax.experimental import pallas as pl
from jax.experimental.pallas import tpu as pltpu
from jax.sharding import Mesh, PartitionSpec as P

BLOCK = 128
TEX_W = 256
ROWS = 1536
OBS = 192
PER = 8
SLOTS = 16
FAR_N = 32
SHARE = TEX_W // FAR_N
WINDOW = 304
BODY = 320
F32 = jnp.float32
VMEM = pl.BlockSpec(memory_space=pltpu.VMEM)
HBM = pl.BlockSpec(memory_space=pltpu.HBM)
SMEM = pl.BlockSpec(memory_space=pltpu.SMEM)


def col_dot(left, right):
    return lax.dot_general(left, right, (((0,), (0,)), ((), ())), preferred_element_type=F32)


def iota(shape, dim):
    return lax.broadcasted_iota(jnp.int32, shape, dim)


def find_starts(obs_ref, starts):
    starts[SLOTS] = OBS

    def step(i, carry):
        j = OBS - 1 - i
        starts[obs_ref[j]] = j
        return carry

    lax.fori_loop(0, OBS, step, 0, unroll=8)


def fetch(pairs, sems):
    copies = []
    for src, dst in pairs:
        if dst.shape[0] != ROWS:
            copies.append(pltpu.make_async_copy(src, dst, sems.at[len(copies)]))
            continue
        for n in range(0, ROWS, ROWS // 4):
            part = pl.ds(n, ROWS // 4)
            copies.append(pltpu.make_async_copy(src.at[part], dst.at[part], sems.at[len(copies)]))
    for copy in copies:
        copy.start()
    return copies


def tex_sums(tex_ref, res_ref, ids_ref, pattern_ref, starts, out_ref):
    obs_index = iota((OBS, BLOCK), 0)
    masks = []
    for bit in range(2):
        keep = jnp.zeros((OBS, BLOCK), jnp.int32)
        for s in range(SLOTS):
            keep = jnp.where(obs_index >= starts[s], (pattern_ref[ids_ref[s]] >> bit) & 1, keep)
        rows = jnp.broadcast_to(keep.astype(F32)[:, None, :], (OBS, PER, BLOCK))
        masks.append(rows.reshape(ROWS, BLOCK).astype(jnp.bfloat16))
    masked = tex_ref[...] * jnp.concatenate(masks, axis=1)
    hess = col_dot(masked, masked)
    grad = jnp.dot(res_ref[...], masked, preferred_element_type=F32)
    h00, h10, h11 = hess[:BLOCK, :BLOCK], hess[BLOCK:, :BLOCK], hess[BLOCK:, BLOCK:]
    row, col = iota((BLOCK, BLOCK), 0), iota((BLOCK, BLOCK), 1)
    mixed = jnp.where(row >= col, h00, h11)
    diag = jnp.sum(jnp.where(row == col, h11, 0.0), axis=0, keepdims=True)
    half = FAR_N // 2
    out_ref[:, SHARE:, :] = jnp.zeros((FAR_N, 8, BLOCK), F32)
    out_ref[:half, :SHARE, :] = mixed.reshape(half, SHARE, BLOCK)
    out_ref[half:, :SHARE, :] = h10.reshape(half, SHARE, BLOCK)
    out_ref[0, SHARE : SHARE + 1, :] = grad[:, :BLOCK]
    out_ref[1, SHARE : SHARE + 1, :] = grad[:, BLOCK:]
    out_ref[2, SHARE : SHARE + 1, :] = diag


def packed(hess):
    row, lane = iota((64, BLOCK), 0), iota((64, BLOCK), 1)
    low, high = hess[64:, :], hess[:64, :]
    turned = pltpu.roll(high, 64, 1)
    pair = jnp.where((lane >= 64) & (row >= lane - 64), turned, low)
    return pair, jnp.sum(jnp.where(row == lane - 64, low, 0.0), axis=0, keepdims=True)


def local_kernel(
    cam_any, tex_any, res_any, obs_any, ids_any, pattern_any, out0, out1, out2, out3, tex_out,
    starts, cam_ref, tex_ref, res_ref, obs_ref, ids_ref, pattern_ref, sems, outs, tex_sums_ref, out_sems,
):
    dests, my_x, my_yl = (out0, out1, out2, out3), lax.axis_index("x"), lax.axis_index("yl")
    copies = fetch(
        (
            (obs_any, obs_ref),
            (ids_any, ids_ref),
            (pattern_any, pattern_ref),
            (res_any, res_ref),
            (cam_any, cam_ref),
            (tex_any, tex_ref),
        ),
        sems,
    )
    for copy in copies[:4]:
        copy.wait()
    find_starts(obs_ref, starts)
    sub = iota((SLOTS, BLOCK), 0)
    first = jnp.zeros((SLOTS, BLOCK), jnp.int32)
    last = jnp.zeros((SLOTS, BLOCK), jnp.int32)
    for copy in copies[4:]:
        copy.wait()
    tex_sums(tex_ref, res_ref, ids_ref, pattern_ref, starts, tex_sums_ref)
    leave = [pltpu.make_async_copy(tex_sums_ref, tex_out, out_sems.at[4])]
    leave[0].start()

    def bounds(k, j):
        slot = ((my_yl + j) & 3) * 4 + ((my_x + k) & 3)
        lo, hi = starts[slot] * PER, starts[slot + 1] * PER
        begin = pl.multiple_of(jnp.minimum((lo >> 4) << 4, ROWS - WINDOW), 16)
        code = pattern_ref[ids_ref[slot]]
        return lo, hi, begin, (code & 1) == 1, (code >> 1) == 1

    def part(begin, lo, hi, count):
        cam = cam_ref[pl.ds(begin, count), :]
        both = jnp.concatenate([cam, tex_ref[pl.ds(begin, count), :]], axis=1)
        where = iota((count, BLOCK), 0) + begin
        keep = ((where >= lo) & (where < hi)).astype(F32).astype(jnp.bfloat16)
        return col_dot(cam * keep, both)

    for i in range(SLOTS):
        lo, hi, *_ = bounds(i // 4, i % 4)
        first = jnp.where(sub == i, lo, first)
        last = jnp.where(sub == i, hi, last)
    lane = iota((SLOTS, ROWS), 1)
    first = jnp.tile(first, (1, ROWS // BLOCK))
    last = jnp.tile(last, (1, ROWS // BLOCK))
    res = jnp.broadcast_to(res_ref[...].astype(F32), (SLOTS, ROWS))
    spread = jnp.where((lane >= first) & (lane < last), res, 0.0).astype(jnp.bfloat16)
    grad = jnp.dot(spread, cam_ref[...], preferred_element_type=F32)
    zero = jnp.zeros((BLOCK, BLOCK), F32)
    for k in (2, 1, 3, 0):
        for j in range(4):
            out, base, tail = outs.at[k], j * BODY, 4 * BODY + 2 * j
            lo, hi, begin, keep0, keep1 = bounds(k, j)
            sums = part(begin, lo, hi, WINDOW)
            pair, diag = packed(sums[:, :BLOCK])
            out[base : base + 128, :] = jnp.where(keep0, sums[:, BLOCK : 2 * BLOCK], zero)
            out[base + 128 : base + 256, :] = jnp.where(keep1, sums[:, 2 * BLOCK :], zero)
            out[base + 256 : base + 320, :] = pair
            out[tail + 1 : tail + 2, :] = diag
            out[tail : tail + 1, :] = grad[4 * k + j : 4 * k + j + 1, :]
        leave.append(pltpu.make_async_copy(outs.at[k], dests[k], out_sems.at[k]))
        leave[-1].start()
    for copy in leave:
        copy.wait()


def near_kernel(a_ref, b_ref, out_ref):
    out_ref[...] = a_ref[...] + b_ref[...]


def add_kernel(a_ref, b_ref, c_ref, *outs):
    for j in range(4):
        for rows, put in (
            (slice(j * BODY, (j + 1) * BODY), slice(0, BODY)),
            (slice(4 * BODY + 2 * j, 4 * BODY + 2 * j + 2), slice(BODY, BODY + 2)),
        ):
            outs[j][put, :] = (a_ref[rows, :] + b_ref[rows, :]) + c_ref[rows, :]
        outs[j][BODY + 2 :, :] = jnp.zeros((6, BLOCK), F32)


def split3(value):
    high = value.astype(jnp.bfloat16)
    return high, (value - high.astype(F32)).astype(jnp.bfloat16)


def near_dot(left, right, dims=((1,), (0,))):
    (lk,), (rk,) = dims
    lh, ll = split3(left)
    rh, rl = split3(right)
    return lax.dot_general(
        jnp.concatenate([lh, lh, ll], axis=lk),
        jnp.concatenate([rh, rl, rh], axis=rk),
        (dims, ((), ())),
        preferred_element_type=F32,
    )


def lanes(value, k):
    return jnp.broadcast_to(value[:, k : k + 1], (8, BLOCK))


def subs(value, j):
    return jnp.broadcast_to(value[j : j + 1, :], (8, BLOCK))


def factor(ab, upper, block):
    row, col = iota((BLOCK, BLOCK), 0), iota((BLOCK, BLOCK), 1)
    sub = iota((8, BLOCK), 0)
    ab[:, :BLOCK] = block
    ab[:, BLOCK:] = (row == col).astype(F32)
    cur = [block[:8], ab[:8, BLOCK:]]
    heads = [lanes(cur[0], k) for k in range(8)]
    for b in range(16):
        more = b < 15
        if more:
            rows = slice(8 * (b + 1), 8 * (b + 2))
            below = [ab[rows, :BLOCK], ab[rows, BLOCK:]]
            tails = [lanes(below[0], 8 * b + k) for k in range(8)]
            later = [lanes(below[0], 8 * (b + 1) + k) for k in range(8)]
        for j in range(8):
            scale = lax.rsqrt(subs(heads[j], j))
            head = jnp.where(sub > j, heads[j] * scale, 0.0)
            for k in range(j + 1, 8):
                pick = subs(heads[k], j) * scale
                heads[k] = heads[k] - head * pick
                if more:
                    if k == j + 1:
                        tail = tails[j] * scale
                    tails[k] = tails[k] - tail * pick
            if more and j == 7:
                tail = tails[j] * scale
            if more:
                later = [value - tail * subs(tail, k) for k, value in enumerate(later)]
            for part in range(2):
                pivot = subs(cur[part], j) * scale
                cur[part] = jnp.where(sub == j, pivot, cur[part] - head * pivot)
                if more:
                    below[part] = below[part] - tail * pivot
        done = jnp.concatenate(cur, axis=1)
        upper[8 * b : 8 * b + 8, :] = done
        if b < 14:
            high, low = split3(done)
            update = col_dot(
                jnp.concatenate([high[:, :BLOCK], high[:, :BLOCK], low[:, :BLOCK]], axis=0),
                jnp.concatenate([high, low, high], axis=0),
            )
            ab[8 * (b + 2) :, :] -= update[8 * (b + 2) :, :]
        if more:
            cur, heads = below, later
    return jnp.where(row >= col, upper[:, :BLOCK].T, 0.0), upper[:, BLOCK:]


def panel_kernel(sums_ref, damping_ref, factor_ref, inv_ref, sol_ref, ab, upper):
    damping = damping_ref[0]
    sums = sums_ref[...]
    both = sums[:, :SHARE, :].reshape(TEX_W, BLOCK)
    mixed, h10 = both[:BLOCK], both[BLOCK:]
    g0, g1, diag = sums[0, SHARE : SHARE + 1, :], sums[1, SHARE : SHARE + 1, :], sums[2, SHARE : SHARE + 1, :]
    row, col = iota((BLOCK, BLOCK), 0), iota((BLOCK, BLOCK), 1)
    flipped = mixed.T
    h00 = jnp.where(row >= col, mixed, flipped)
    h11 = jnp.where(row < col, mixed, jnp.where(row == col, diag, flipped))
    h00 = jnp.where(row == col, h00 + damping * h00, h00)
    h11 = jnp.where(row == col, h11 + damping * h11, h11)
    across = ((1,), (1,))
    l00, w00 = factor(ab, upper, h00)
    l10 = near_dot(h10, w00, across)
    y0 = near_dot(g0, w00, across)
    zero = jnp.zeros((BLOCK, BLOCK), F32)
    factor_ref[:BLOCK, :BLOCK] = l00
    factor_ref[:BLOCK, BLOCK:] = zero
    factor_ref[BLOCK:, :BLOCK] = l10
    inv_ref[:BLOCK, :BLOCK] = w00
    inv_ref[:BLOCK, BLOCK:] = zero
    lw = near_dot(l10, w00)
    l11, w11 = factor(ab, upper, h11 - near_dot(l10, l10, across))
    factor_ref[BLOCK:, BLOCK:] = l11
    inv_ref[BLOCK:, :BLOCK] = -near_dot(w11, lw)
    inv_ref[BLOCK:, BLOCK:] = w11
    sol_ref[:, :BLOCK] = y0
    sol_ref[:, BLOCK:] = near_dot(g1 - near_dot(y0, l10, across), w11, across)


def last_kernel(a_ref, b_ref, c_ref, d_ref, inv_ref, sol_ref, damping_ref, red_ref, grad_ref, coup_ref):
    damping = damping_ref[0]
    total = (a_ref[...] + b_ref[...]) + (c_ref[...] + d_ref[...])
    cross = jnp.concatenate([total[:128], total[128:256]], axis=1)
    pair, grad, diag = total[256:320], total[320:321], total[321:322]
    row, col = iota((BLOCK, BLOCK), 0), iota((BLOCK, BLOCK), 1)
    row64, lane64 = iota((64, BLOCK), 0), iota((64, BLOCK), 1)
    turned = pltpu.roll(pair, 64, 1)
    top = jnp.where(lane64 < 64, turned, 0.0)
    square = jnp.concatenate([top, pair], axis=0)
    other = square.T
    lower = jnp.where((row >= 64) & (col >= 64), other, square)
    lower = jnp.where(row > col, lower, 0.0)
    main = jnp.where(row == col, jnp.where(row < 64, square, diag), 0.0)
    hess = lower + lower.T + main + damping * main
    coupling = near_dot(cross, inv_ref[...], ((1,), (1,)))
    coup_ref[...] = coupling
    red_ref[...] = hess - near_dot(coupling, coupling, ((1,), (1,)))
    grad_ref[...] = grad - near_dot(sol_ref[...], coupling, ((1,), (1,)))


LOCAL_SCRATCH = [
    pltpu.SMEM((SLOTS + 1,), jnp.int32),
    pltpu.VMEM((ROWS, BLOCK), jnp.bfloat16),
    pltpu.VMEM((ROWS, TEX_W), jnp.bfloat16),
    pltpu.VMEM((1, ROWS), jnp.bfloat16),
    pltpu.SMEM((OBS,), jnp.int32),
    pltpu.SMEM((SLOTS,), jnp.int32),
    pltpu.SMEM((512,), jnp.int32),
    pltpu.SemaphoreType.DMA((12,)),
    pltpu.VMEM((4, 4 * BODY + 8, BLOCK), F32),
    pltpu.VMEM((FAR_N, 2 * SHARE, BLOCK), F32),
    pltpu.SemaphoreType.DMA((5,)),
]
COST = {
    name: pl.CostEstimate(flops=flops, bytes_accessed=0, transcendentals=0)
    for name, flops in {"near": 300000000, "add": 500000000}.items()
}
PANEL = [pltpu.VMEM((BLOCK, TEX_W), F32), pltpu.VMEM((BLOCK, TEX_W), F32)]


def call(kernel, name, outs, specs, scratch=(), room=24, out_spec=VMEM):
    return pl.pallas_call(
        kernel,
        cost_estimate=COST.get(name),
        out_shape=[jax.ShapeDtypeStruct(s, F32) for s in outs],
        in_specs=specs,
        out_specs=[out_spec] * len(outs),
        scratch_shapes=scratch,
        name=name,
        compiler_params=pltpu.CompilerParams(vmem_limit_bytes=room * 2**20),
    )


def shift(value, axis, by):
    n = lax.axis_size(axis)
    return lax.ppermute(value, axis, [(i, (i + by) % n) for i in range(n)])


def spread_sum(value, axes):
    count = lax.axis_size(axes)
    copies = jnp.broadcast_to(value[None], (count, *value.shape))
    return jnp.sum(lax.all_to_all(copies, axes, 0, 0), axis=0)


FAR = ("x", "z")
NEAR = ("yl", "yh", "c")


def shards(jac_cam, jac_tex, residual, obs_slot, col_ids, block_pattern, damping):
    cam, tex = jac_cam[0, 0], jac_tex[0, 0]
    res, obs = residual[0], obs_slot[0, 0]
    damping = damping.reshape(1)

    *pieces, tex_part = call(
        local_kernel,
        "local",
        [(4 * BODY + 8, BLOCK)] * 4 + [(FAR_N, SHARE + 8, BLOCK)],
        [HBM] * 6,
        LOCAL_SCRATCH,
        60,
        HBM,
    )(cam, tex, res, obs, col_ids, block_pattern)
    far, right, left = (shift(pieces[k], "x", k) for k in (2, 1, 3))
    (near,) = call(near_kernel, "near", [(4 * BODY + 8, BLOCK)], [VMEM] * 2)(pieces[0], far)
    pieces = call(add_kernel, "add", [(BODY + 8, BLOCK)] * 4, [VMEM] * 3)(near, right, left)
    parts = [pieces[0]] + [shift(pieces[j], "yl", j) for j in (2, 1, 3)]

    share = jnp.sum(lax.all_to_all(tex_part, FAR, 0, 0), axis=0)
    share = spread_sum(share, NEAR)
    copies = jnp.broadcast_to(share[None], (FAR_N, *share.shape))
    tex_sums = lax.all_to_all(copies, FAR, 0, 0)

    texture_factor, inverse, sol = call(
        panel_kernel, "panel", [(TEX_W, TEX_W), (TEX_W, TEX_W), (1, TEX_W)], [VMEM, SMEM], PANEL
    )(tex_sums, damping)
    reduced, gradient, coupling = call(
        last_kernel,
        "last",
        [(BLOCK, BLOCK), (1, BLOCK), (BLOCK, TEX_W)],
        [VMEM] * 6 + [SMEM],
    )(*parts, inverse, sol, damping)
    return (reduced[None, None], gradient[None], coupling[None, None], texture_factor)


def solution(mesh):
    fine = Mesh(mesh.devices.reshape(4, 4, 2, 8, 2), ("yl", "x", "yh", "z", "c"))
    img, blk = ("yl", "x"), ("yh", "z", "c")
    return jax.shard_map(
        shards,
        mesh=fine,
        in_specs=(
            P(img, blk, None, None),
            P(img, blk, None, None),
            P(img, blk, None),
            P(img, blk, None),
            P(blk),
            P(),
            P(),
        ),
        out_specs=(
            P(blk, img, None, None),
            P(blk, img, None),
            P(blk, img, None, None),
            P(),
        ),
        check_vma=False,
    )
```

```python
import functools

import jax
import jax.numpy as jnp
from jax import lax
from jax.experimental import pallas as pl
from jax.experimental.pallas import tpu as pltpu
from jax.sharding import Mesh, PartitionSpec as P

BLOCK = 128
TEX_W = 256
ROWS = 1536
OBS = 192
PER = 8
SLOTS = 16
FAR_N = 32
SHARE = TEX_W // FAR_N
WINDOW = 304
BODY = 320
F32 = jnp.float32
VMEM = pl.BlockSpec(memory_space=pltpu.VMEM)
HBM = pl.BlockSpec(memory_space=pltpu.HBM)
SMEM = pl.BlockSpec(memory_space=pltpu.SMEM)


def col_dot(left, right):
    return lax.dot_general(left, right, (((0,), (0,)), ((), ())), preferred_element_type=F32)


def iota(shape, dim):
    return lax.broadcasted_iota(jnp.int32, shape, dim)


def find_starts(obs_ref, starts):
    starts[SLOTS] = OBS

    def step(i, carry):
        j = OBS - 1 - i
        starts[obs_ref[j]] = j
        return carry

    lax.fori_loop(0, OBS, step, 0, unroll=8)


def fetch(pairs, sems):
    copies = []
    for src, dst in pairs:
        if dst.shape[0] != ROWS:
            copies.append(pltpu.make_async_copy(src, dst, sems.at[len(copies)]))
            continue
        for n in range(0, ROWS, ROWS // 4):
            part = pl.ds(n, ROWS // 4)
            copies.append(pltpu.make_async_copy(src.at[part], dst.at[part], sems.at[len(copies)]))
    for copy in copies:
        copy.start()
    return copies


def tex_sums(tex_ref, res_ref, ids_ref, pattern_ref, starts, out_ref):
    obs_index = iota((OBS, BLOCK), 0)
    masks = []
    for bit in range(2):
        keep = jnp.zeros((OBS, BLOCK), jnp.int32)
        for s in range(SLOTS):
            keep = jnp.where(obs_index >= starts[s], (pattern_ref[ids_ref[s]] >> bit) & 1, keep)
        rows = jnp.broadcast_to(keep.astype(F32)[:, None, :], (OBS, PER, BLOCK))
        masks.append(rows.reshape(ROWS, BLOCK).astype(jnp.bfloat16))
    masked = tex_ref[...] * jnp.concatenate(masks, axis=1)
    hess = col_dot(masked, masked)
    grad = jnp.dot(res_ref[...], masked, preferred_element_type=F32)
    h00, h10, h11 = hess[:BLOCK, :BLOCK], hess[BLOCK:, :BLOCK], hess[BLOCK:, BLOCK:]
    row, col = iota((BLOCK, BLOCK), 0), iota((BLOCK, BLOCK), 1)
    mixed = jnp.where(row >= col, h00, h11)
    diag = jnp.sum(jnp.where(row == col, h11, 0.0), axis=0, keepdims=True)
    half = FAR_N // 2
    out_ref[:, SHARE:, :] = jnp.zeros((FAR_N, 8, BLOCK), F32)
    out_ref[:half, :SHARE, :] = mixed.reshape(half, SHARE, BLOCK)
    out_ref[half:, :SHARE, :] = h10.reshape(half, SHARE, BLOCK)
    out_ref[0, SHARE : SHARE + 1, :] = grad[:, :BLOCK]
    out_ref[1, SHARE : SHARE + 1, :] = grad[:, BLOCK:]
    out_ref[2, SHARE : SHARE + 1, :] = diag


def packed(hess):
    row, lane = iota((64, BLOCK), 0), iota((64, BLOCK), 1)
    low, high = hess[64:, :], hess[:64, :]
    turned = pltpu.roll(high, 64, 1)
    pair = jnp.where((lane >= 64) & (row >= lane - 64), turned, low)
    return pair, jnp.sum(jnp.where(row == lane - 64, low, 0.0), axis=0, keepdims=True)


def local_kernel(
    cam_any, tex_any, res_any, obs_any, ids_any, pattern_any, out0, out1, out2, out3, tex_out,
    starts, cam_ref, tex_ref, res_ref, obs_ref, ids_ref, pattern_ref, sems, outs, tex_sums_ref, out_sems,
):
    dests, my_x, my_yl = (out0, out1, out2, out3), lax.axis_index("x"), lax.axis_index("yl")
    copies = fetch(
        (
            (obs_any, obs_ref),
            (ids_any, ids_ref),
            (pattern_any, pattern_ref),
            (res_any, res_ref),
            (cam_any, cam_ref),
            (tex_any, tex_ref),
        ),
        sems,
    )
    copies[0].wait()
    find_starts(obs_ref, starts)
    for copy in copies[1:4]:
        copy.wait()
    sub = iota((SLOTS, BLOCK), 0)
    first = jnp.zeros((SLOTS, BLOCK), jnp.int32)
    last = jnp.zeros((SLOTS, BLOCK), jnp.int32)
    for copy in copies[4:]:
        copy.wait()
    tex_sums(tex_ref, res_ref, ids_ref, pattern_ref, starts, tex_sums_ref)
    leave = [pltpu.make_async_copy(tex_sums_ref, tex_out, out_sems.at[4])]
    leave[0].start()

    def bounds(k, j):
        slot = ((my_yl + j) & 3) * 4 + ((my_x + k) & 3)
        lo, hi = starts[slot] * PER, starts[slot + 1] * PER
        begin = pl.multiple_of(jnp.minimum((lo >> 4) << 4, ROWS - WINDOW), 16)
        code = pattern_ref[ids_ref[slot]]
        return lo, hi, begin, (code & 1) == 1, (code >> 1) == 1

    def part(begin, lo, hi, count):
        cam = cam_ref[pl.ds(begin, count), :]
        both = jnp.concatenate([cam, tex_ref[pl.ds(begin, count), :]], axis=1)
        where = iota((count, BLOCK), 0) + begin
        keep = ((where >= lo) & (where < hi)).astype(F32).astype(jnp.bfloat16)
        return col_dot(cam * keep, both)

    for i in range(SLOTS):
        lo, hi, *_ = bounds(i // 4, i % 4)
        first = jnp.where(sub == i, lo, first)
        last = jnp.where(sub == i, hi, last)
    lane = iota((SLOTS, ROWS), 1)
    first = jnp.tile(first, (1, ROWS // BLOCK))
    last = jnp.tile(last, (1, ROWS // BLOCK))
    res = jnp.broadcast_to(res_ref[...].astype(F32), (SLOTS, ROWS))
    spread = jnp.where((lane >= first) & (lane < last), res, 0.0).astype(jnp.bfloat16)
    grad = jnp.dot(spread, cam_ref[...], preferred_element_type=F32)
    zero = jnp.zeros((BLOCK, BLOCK), F32)
    for k in (2, 1, 3, 0):
        for j in range(4):
            out, base, tail = outs.at[k], j * BODY, 4 * BODY + 2 * j
            lo, hi, begin, keep0, keep1 = bounds(k, j)
            sums = part(begin, lo, hi, WINDOW)
            pair, diag = packed(sums[:, :BLOCK])
            out[base : base + 128, :] = jnp.where(keep0, sums[:, BLOCK : 2 * BLOCK], zero)
            out[base + 128 : base + 256, :] = jnp.where(keep1, sums[:, 2 * BLOCK :], zero)
            out[base + 256 : base + 320, :] = pair
            out[tail + 1 : tail + 2, :] = diag
            out[tail : tail + 1, :] = grad[4 * k + j : 4 * k + j + 1, :]
        leave.append(pltpu.make_async_copy(outs.at[k], dests[k], out_sems.at[k]))
        leave[-1].start()
    for copy in leave:
        copy.wait()


def near_kernel(a_ref, b_ref, out_ref):
    out_ref[...] = a_ref[...] + b_ref[...]


def add_kernel(a_ref, b_ref, c_ref, *outs):
    for j in range(4):
        for rows, put in (
            (slice(j * BODY, (j + 1) * BODY), slice(0, BODY)),
            (slice(4 * BODY + 2 * j, 4 * BODY + 2 * j + 2), slice(BODY, BODY + 2)),
        ):
            outs[j][put, :] = (a_ref[rows, :] + b_ref[rows, :]) + c_ref[rows, :]
        outs[j][BODY + 2 :, :] = jnp.zeros((6, BLOCK), F32)


def split3(value):
    high = value.astype(jnp.bfloat16)
    return high, (value - high.astype(F32)).astype(jnp.bfloat16)


def near_dot(left, right, dims=((1,), (0,))):
    (lk,), (rk,) = dims
    lh, ll = split3(left)
    rh, rl = split3(right)
    return lax.dot_general(
        jnp.concatenate([lh, lh, ll], axis=lk),
        jnp.concatenate([rh, rl, rh], axis=rk),
        (dims, ((), ())),
        preferred_element_type=F32,
    )


def lanes(value, k):
    return jnp.broadcast_to(value[:, k : k + 1], (8, BLOCK))


def subs(value, j):
    return jnp.broadcast_to(value[j : j + 1, :], (8, BLOCK))


def factor(ab, upper, block):
    row, col = iota((BLOCK, BLOCK), 0), iota((BLOCK, BLOCK), 1)
    sub = iota((8, BLOCK), 0)
    ab[:, :BLOCK] = block
    ab[:, BLOCK:] = (row == col).astype(F32)
    cur = [block[:8], ab[:8, BLOCK:]]
    heads = [lanes(cur[0], k) for k in range(8)]
    for b in range(16):
        more = b < 15
        if more:
            rows = slice(8 * (b + 1), 8 * (b + 2))
            below = [ab[rows, :BLOCK], ab[rows, BLOCK:]]
            tails = [lanes(below[0], 8 * b + k) for k in range(8)]
            later = [lanes(below[0], 8 * (b + 1) + k) for k in range(8)]
        for j in range(8):
            scale = lax.rsqrt(subs(heads[j], j))
            head = jnp.where(sub > j, heads[j] * scale, 0.0)
            for k in range(j + 1, 8):
                pick = subs(heads[k], j) * scale
                heads[k] = heads[k] - head * pick
                if more:
                    if k == j + 1:
                        tail = tails[j] * scale
                    tails[k] = tails[k] - tail * pick
            if more and j == 7:
                tail = tails[j] * scale
            if more:
                later = [value - tail * subs(tail, k) for k, value in enumerate(later)]
            for part in range(2):
                pivot = subs(cur[part], j) * scale
                cur[part] = jnp.where(sub == j, pivot, cur[part] - head * pivot)
                if more:
                    below[part] = below[part] - tail * pivot
        done = jnp.concatenate(cur, axis=1)
        upper[8 * b : 8 * b + 8, :] = done
        if b < 14:
            high, low = split3(done)
            update = col_dot(
                jnp.concatenate([high[:, :BLOCK], high[:, :BLOCK], low[:, :BLOCK]], axis=0),
                jnp.concatenate([high, low, high], axis=0),
            )
            ab[8 * (b + 2) :, :] -= update[8 * (b + 2) :, :]
        if more:
            cur, heads = below, later
    return jnp.where(row >= col, upper[:, :BLOCK].T, 0.0), upper[:, BLOCK:]


def panel_kernel(sums_ref, damping_ref, factor_ref, inv_ref, sol_ref, ab, upper):
    damping = damping_ref[0]
    sums = sums_ref[...]
    both = sums[:, :SHARE, :].reshape(TEX_W, BLOCK)
    mixed, h10 = both[:BLOCK], both[BLOCK:]
    g0, g1, diag = sums[0, SHARE : SHARE + 1, :], sums[1, SHARE : SHARE + 1, :], sums[2, SHARE : SHARE + 1, :]
    row, col = iota((BLOCK, BLOCK), 0), iota((BLOCK, BLOCK), 1)
    flipped = mixed.T
    h00 = jnp.where(row >= col, mixed, flipped)
    h11 = jnp.where(row < col, mixed, jnp.where(row == col, diag, flipped))
    h00 = jnp.where(row == col, h00 + damping * h00, h00)
    h11 = jnp.where(row == col, h11 + damping * h11, h11)
    across = ((1,), (1,))
    l00, w00 = factor(ab, upper, h00)
    l10 = near_dot(h10, w00, across)
    y0 = near_dot(g0, w00, across)
    zero = jnp.zeros((BLOCK, BLOCK), F32)
    factor_ref[:BLOCK, :BLOCK] = l00
    factor_ref[:BLOCK, BLOCK:] = zero
    factor_ref[BLOCK:, :BLOCK] = l10
    inv_ref[:BLOCK, :BLOCK] = w00
    inv_ref[:BLOCK, BLOCK:] = zero
    lw = near_dot(l10, w00)
    l11, w11 = factor(ab, upper, h11 - near_dot(l10, l10, across))
    factor_ref[BLOCK:, BLOCK:] = l11
    inv_ref[BLOCK:, :BLOCK] = -near_dot(w11, lw)
    inv_ref[BLOCK:, BLOCK:] = w11
    sol_ref[:, :BLOCK] = y0
    sol_ref[:, BLOCK:] = near_dot(g1 - near_dot(y0, l10, across), w11, across)


def last_kernel(a_ref, b_ref, c_ref, d_ref, inv_ref, sol_ref, damping_ref, red_ref, grad_ref, coup_ref):
    damping = damping_ref[0]
    total = (a_ref[...] + b_ref[...]) + (c_ref[...] + d_ref[...])
    cross = jnp.concatenate([total[:128], total[128:256]], axis=1)
    pair, grad, diag = total[256:320], total[320:321], total[321:322]
    row, col = iota((BLOCK, BLOCK), 0), iota((BLOCK, BLOCK), 1)
    row64, lane64 = iota((64, BLOCK), 0), iota((64, BLOCK), 1)
    turned = pltpu.roll(pair, 64, 1)
    top = jnp.where(lane64 < 64, turned, 0.0)
    square = jnp.concatenate([top, pair], axis=0)
    other = square.T
    lower = jnp.where((row >= 64) & (col >= 64), other, square)
    lower = jnp.where(row > col, lower, 0.0)
    main = jnp.where(row == col, jnp.where(row < 64, square, diag), 0.0)
    hess = lower + lower.T + main + damping * main
    coupling = near_dot(cross, inv_ref[...], ((1,), (1,)))
    coup_ref[...] = coupling
    red_ref[...] = hess - near_dot(coupling, coupling, ((1,), (1,)))
    grad_ref[...] = grad - near_dot(sol_ref[...], coupling, ((1,), (1,)))


LOCAL_SCRATCH = [
    pltpu.SMEM((SLOTS + 1,), jnp.int32),
    pltpu.VMEM((ROWS, BLOCK), jnp.bfloat16),
    pltpu.VMEM((ROWS, TEX_W), jnp.bfloat16),
    pltpu.VMEM((1, ROWS), jnp.bfloat16),
    pltpu.SMEM((OBS,), jnp.int32),
    pltpu.SMEM((SLOTS,), jnp.int32),
    pltpu.SMEM((512,), jnp.int32),
    pltpu.SemaphoreType.DMA((12,)),
    pltpu.VMEM((4, 4 * BODY + 8, BLOCK), F32),
    pltpu.VMEM((FAR_N, 2 * SHARE, BLOCK), F32),
    pltpu.SemaphoreType.DMA((5,)),
]
COST = {
    name: pl.CostEstimate(flops=flops, bytes_accessed=0, transcendentals=0)
    for name, flops in {"near": 300000000, "add": 500000000}.items()
}
PANEL = [pltpu.VMEM((BLOCK, TEX_W), F32), pltpu.VMEM((BLOCK, TEX_W), F32)]


def call(kernel, name, outs, specs, scratch=(), room=24, out_spec=VMEM):
    return pl.pallas_call(
        kernel,
        cost_estimate=COST.get(name),
        out_shape=[jax.ShapeDtypeStruct(s, F32) for s in outs],
        in_specs=specs,
        out_specs=[out_spec] * len(outs),
        scratch_shapes=scratch,
        name=name,
        compiler_params=pltpu.CompilerParams(vmem_limit_bytes=room * 2**20),
    )


def shift(value, axis, by):
    n = lax.axis_size(axis)
    return lax.ppermute(value, axis, [(i, (i + by) % n) for i in range(n)])


def spread_sum(value, axes):
    count = lax.axis_size(axes)
    copies = jnp.broadcast_to(value[None], (count, *value.shape))
    return jnp.sum(lax.all_to_all(copies, axes, 0, 0), axis=0)


FAR = ("x", "z")
NEAR = ("yl", "yh", "c")


def shards(jac_cam, jac_tex, residual, obs_slot, col_ids, block_pattern, damping):
    cam, tex = jac_cam[0, 0], jac_tex[0, 0]
    res, obs = residual[0], obs_slot[0, 0]
    damping = damping.reshape(1)

    *pieces, tex_part = call(
        local_kernel,
        "local",
        [(4 * BODY + 8, BLOCK)] * 4 + [(FAR_N, SHARE + 8, BLOCK)],
        [HBM] * 6,
        LOCAL_SCRATCH,
        60,
        HBM,
    )(cam, tex, res, obs, col_ids, block_pattern)
    far, right, left = (shift(pieces[k], "x", k) for k in (2, 1, 3))
    (near,) = call(near_kernel, "near", [(4 * BODY + 8, BLOCK)], [VMEM] * 2)(pieces[0], far)
    pieces = call(add_kernel, "add", [(BODY + 8, BLOCK)] * 4, [VMEM] * 3)(near, right, left)
    parts = [pieces[0]] + [shift(pieces[j], "yl", j) for j in (2, 1, 3)]

    share = jnp.sum(lax.all_to_all(tex_part, FAR, 0, 0), axis=0)
    share = spread_sum(share, NEAR)
    copies = jnp.broadcast_to(share[None], (FAR_N, *share.shape))
    tex_sums = lax.all_to_all(copies, FAR, 0, 0)

    texture_factor, inverse, sol = call(
        panel_kernel, "panel", [(TEX_W, TEX_W), (TEX_W, TEX_W), (1, TEX_W)], [VMEM, SMEM], PANEL
    )(tex_sums, damping)
    reduced, gradient, coupling = call(
        last_kernel,
        "last",
        [(BLOCK, BLOCK), (1, BLOCK), (BLOCK, TEX_W)],
        [VMEM] * 6 + [SMEM],
    )(*parts, inverse, sol, damping)
    return (reduced[None, None], gradient[None], coupling[None, None], texture_factor)


def solution(mesh):
    fine = Mesh(mesh.devices.reshape(4, 4, 2, 8, 2), ("yl", "x", "yh", "z", "c"))
    img, blk = ("yl", "x"), ("yh", "z", "c")
    return jax.shard_map(
        shards,
        mesh=fine,
        in_specs=(
            P(img, blk, None, None),
            P(img, blk, None, None),
            P(img, blk, None),
            P(img, blk, None),
            P(blk),
            P(),
            P(),
        ),
        out_specs=(
            P(blk, img, None, None),
            P(blk, img, None),
            P(blk, img, None, None),
            P(),
        ),
        check_vma=False,
    )
```
